32 devices in a mesh: seq: 4 (over x, core), ctx: 8 (over z, y).
Axes of the slice: x: 2, y: 2, z: 4, core: 2. Of those that a mesh axis runs over, the one named last changes fastest.
Arguments:
- grad_out: bfloat16 [4, 1024, 4096], P('seq', 'ctx'), may hold values from -6 to 6
- inputs: bfloat16 [4, 1024, 4096], P('seq', 'ctx'), may hold values from -6 to 6
- residues: float32 [16, 256], replicated, may hold values from -4 to 4
- rates: float32 [16, 256], replicated, may hold values from 9.765625e-05 to 0.0625
Outputs:
- grad_in: float32 [4, 1024, 4096], P('seq', 'ctx')
- grad_residues: float32 [16, 256], replicated
The draws below stay inside these ranges and needn't reach their ends.
All inputs are finite; a program needn't handle non-finite values.
Results may differ from the reference program's by a relative error of at most 0.0003.
Values sent between devices are 32-bit elements; how exact they have to be, the bound alone decides.
A program may use at most 128 MiB of HBM per device.

```python
import jax
import jax.numpy as jnp
from jax import lax

D = 4096
G = 256
CG = 16
MODES = 16
TOKENS = 1024
SEQS = 4


def draw_rates(key, part):
    base_key = jax.random.fold_in(key, 11)
    coin_key, slow_key, fast_key = jax.random.split(base_key, 3)
    slow_unit = jax.random.uniform(slow_key, (MODES, G), jnp.float32)
    fast_unit = jax.random.uniform(fast_key, (MODES, G), jnp.float32)
    slow_low = jnp.log(0.25 / TOKENS)
    middle = jnp.log(2.3 / TOKENS)
    fast_high = jnp.log(0.0625)
    slow_rate = jnp.exp(slow_low + slow_unit * (middle - slow_low))
    fast_rate = jnp.exp(middle + fast_unit * (fast_high - middle))
    coin = jax.random.randint(coin_key, (MODES, G), 0, 2, dtype=jnp.int32)
    return jnp.where(coin == 1, slow_rate, fast_rate).astype(jnp.float32)


def block_scale(key, shape, pieces, low, high):
    level, own = 1.0, jax.random.fold_in(key, 6)
    for dim, parts in pieces:
        heights = jnp.exp(jax.random.uniform(jax.random.fold_in(own, dim), (parts,), jnp.float32, low / len(pieces), high / len(pieces)))
        level = level * jnp.repeat(heights, shape[dim] // parts).reshape([-1 if axis == dim else 1 for axis in range(len(shape))])
    return level


def noise(key, dims, width, limit, pieces=(), held_as=jnp.bfloat16):
    array = width * jax.random.normal(key, dims, jnp.float32)
    if pieces:
        array = array * block_scale(key, dims, pieces, -0.22, 0.18)
    return jnp.clip(array, -limit, limit).astype(held_as)


def setup_inputs(seed: int = 0) -> dict:
    arg_keys = jax.random.split(jax.random.key(seed), 5)
    grad_out = noise(arg_keys[0], (SEQS, TOKENS, D), 1.0, 6.0, ((0, 4), (1, 8)))
    inputs = noise(arg_keys[1], (SEQS, TOKENS, D), 1.0, 6.0, ((0, 4), (1, 8)))
    residues = noise(arg_keys[2], (MODES, G), 1.0, 4.0, (), jnp.float32)
    rates = draw_rates(jax.random.fold_in(arg_keys[4], 71), 0)
    return dict(grad_out=grad_out, inputs=inputs, residues=residues, rates=rates)


def reference(grad_out, inputs, residues, rates):
    fft_len = 2 * TOKENS
    chan_block = CG * min(G, 16)
    group_block = chan_block // CG
    lag_axis = jnp.arange(TOKENS, dtype=jnp.float32)
    amplitude = residues * jnp.sqrt(-jnp.expm1(-2.0 * rates) / MODES)
    kernel = jnp.zeros((TOKENS, G), jnp.float32)
    for which in range(MODES):
        kernel = kernel + amplitude[which][None, :] * jnp.exp(-rates[which][None, :] * lag_axis[:, None])
    spectrum = jnp.fft.rfft(kernel, n=fft_len, axis=0)

    def one_block(position):
        first_chan = (position * chan_block).astype(jnp.int32)
        first_group = (position * group_block).astype(jnp.int32)
        grad_block = lax.dynamic_slice_in_dim(grad_out, first_chan, chan_block, 2).astype(jnp.float32)
        input_block = lax.dynamic_slice_in_dim(inputs, first_chan, chan_block, 2).astype(jnp.float32)
        grad_freq = jnp.fft.rfft(grad_block, n=fft_len, axis=1)
        input_freq = jnp.fft.rfft(input_block, n=fft_len, axis=1)
        group_freq = lax.dynamic_slice_in_dim(spectrum, first_group, group_block, 1)
        chan_freq = jnp.repeat(group_freq, CG, axis=1)
        grad_rows = jnp.fft.irfft(jnp.conj(chan_freq)[None] * grad_freq, n=fft_len, axis=1)[:, :TOKENS]
        cross = (jnp.conj(input_freq) * grad_freq).reshape(SEQS, -1, group_block, CG).sum(axis=(0, 3))
        lagged = jnp.fft.irfft(cross, n=fft_len, axis=0)[:TOKENS]
        return (grad_rows, lagged)
    grad_blocks, lag_blocks = lax.map(one_block, jnp.arange(D // chan_block, dtype=jnp.int32))
    grad_in = jnp.moveaxis(grad_blocks, 0, 2).reshape(SEQS, TOKENS, D)
    lag_all = jnp.moveaxis(lag_blocks, 0, 1).reshape(TOKENS, G)
    sums = jnp.stack([lax.optimization_barrier(jnp.sum(jnp.exp(-rates[which][None, :] * lag_axis[:, None]) * lag_all, axis=0)) for which in range(MODES)])
    factor = jnp.sqrt(-jnp.expm1(-2.0 * rates) / float(SEQS * TOKENS * CG))
    return (grad_in, sums * factor)
```

```python
import functools

import jax
import jax.numpy as jnp
from jax import lax
from jax.experimental import pallas as pl
from jax.experimental.pallas import tpu as pltpu
from jax.sharding import PartitionSpec as P

MESH = pl.DeviceIdType.MESH
F32 = jnp.float32
BF16 = jnp.bfloat16


def dot(a, b):
    return jnp.dot(a, b, preferred_element_type=F32)


def split(a):
    high = a.astype(BF16)
    return high, (a - high.astype(F32)).astype(BF16)


def one_minus_exp(u):
    series = 1.0 - u * (1.0 / 8.0)
    for order in (7.0, 6.0, 5.0, 4.0, 3.0, 2.0):
        series = 1.0 - u * (1.0 / order) * series
    return u * series


def body(
    shards, seqs, chunks, grad_ref, in_ref, res_ref, rate_ref, out_ref, total_ref,
    own, pair, joined, incoming, outgoing, decay_pow, decay, tail_high, tail_low, tail, lag_sums,
    partial, from_seq, seq_sum, from_ctx,
    pair_send, pair_recv, chain_send, chain_recv, seq_send, seq_recv, ctx_send, ctx_recv,
):
    rows, width = grad_ref.shape
    modes, groups = res_ref.shape
    per_group = width // groups
    tile_groups = modes if modes * per_group == 256 else 256 // per_group
    tile = tile_groups * per_group
    tiles = width // tile
    chunk_tiles = tiles // chunks
    half = 128
    half_groups = half // per_group
    stacked = tile_groups * modes
    pairs = shards // 2

    me = lax.axis_index("ctx")
    my_seq = lax.axis_index("seq")
    upper = me % 2
    place = me // 2
    partner = me + 1 - 2 * upper
    hops = pairs - 1 - place

    barrier = pltpu.get_barrier_semaphore()
    for offset in range(1, shards):
        pl.semaphore_signal(
            barrier, inc=1, device_id={"ctx": lax.rem(me + offset, shards)}, device_id_type=MESH
        )
    for offset in range(1, seqs):
        pl.semaphore_signal(
            barrier, inc=1, device_id={"seq": lax.rem(my_seq + offset, seqs)}, device_id_type=MESH
        )

    lane_group = lax.broadcasted_iota(jnp.int32, (modes, tile), 1) // per_group
    ahead = lax.broadcasted_iota(jnp.int32, (modes, rows), 1).astype(F32)
    behind = float(rows) - ahead

    def rolled(values, index):
        return pltpu.roll(values, lax.rem(groups - index * tile_groups, groups), 1)

    def compress(wide):
        kept = jnp.zeros((modes, tile), F32)
        for g in range(tile_groups):
            kept = jnp.where(lane_group == g, wide[g * modes : (g + 1) * modes, :], kept)
        return kept

    def lanes(index, size):
        return pl.ds(pl.multiple_of(index * size, size), size)

    def pair_copy(q):
        return pltpu.make_async_remote_copy(
            own.at[q], pair.at[q], pair_send.at[q], pair_recv.at[q],
            device_id={"ctx": partner}, device_id_type=MESH,
        )

    def chain_copy(q):
        return pltpu.make_async_remote_copy(
            outgoing.at[q], incoming.at[q], chain_send.at[q], chain_recv.at[q],
            device_id={"ctx": lax.rem(me + shards - 2, shards)}, device_id_type=MESH,
        )

    for q in range(chunks):
        def summarize(step, carry, q=q):
            index = q * chunk_tiles + step
            rates = rolled(rate_ref[...], index)
            spread = jnp.zeros((modes, tile), F32)
            parts = []
            for g in range(tile_groups):
                rate = rates[:, g : g + 1]
                parts.append(jnp.exp(-rate * ahead))
                spread = jnp.where(lane_group == g, rate, spread)
            decays = jnp.concatenate(parts, axis=0)
            decay[lanes(index, stacked), :] = decays
            high, low = split(decays)
            grads = grad_ref[:, lanes(index, tile)]
            wide = dot(jnp.concatenate([high, low], axis=1), jnp.concatenate([grads, grads], axis=0))
            own[q, :, lanes(step, tile)] = compress(wide)
            decay_pow[q, :, lanes(step, tile)] = jnp.exp(-float(rows) * spread)
            return carry

        lax.fori_loop(0, chunk_tiles, summarize, 0)
        if q == 0:
            pl.semaphore_wait(barrier, shards - 1 + seqs - 1)
        pair_copy(q).start()

    def exchange(step):
        @pl.when(step < chunks)
        def _():
            pair_copy(step).wait_recv()
            power = decay_pow[step]
            mine, other = own[step], pair[step]
            near = jnp.where(upper == 0, mine, other)
            far = jnp.where(upper == 0, other, mine)
            joined[step] = near + power * far

            @pl.when(hops == 0)
            def _():
                incoming[step] = jnp.zeros(incoming.shape[1:], F32)
                if pairs > 1:
                    outgoing[step] = joined[step]
                    chain_copy(step).start()

        if pairs > 1:
            q = step - hops

            @pl.when((hops > 0) & (q >= 0) & (q < chunks))
            def _():
                chain_copy(q).wait_recv()

                @pl.when(place > 0)
                def _():
                    power = decay_pow[q]
                    outgoing[q] = joined[q] + power * power * incoming[q]
                    chain_copy(q).start()

    steps = chunks + pairs - 1
    per_step = max(1, tiles // steps)

    half_lane_group = lax.broadcasted_iota(jnp.int32, (rows, half), 1) // per_group
    row_of = lax.broadcasted_iota(jnp.int32, (rows, rows), 0)
    col_of = lax.broadcasted_iota(jnp.int32, (rows, rows), 1)
    causal = col_of >= row_of
    inside = col_of <= row_of
    reverse = jnp.where(row_of + col_of == rows - 1, 1.0, 0.0).astype(BF16)
    group_lane = lax.broadcasted_iota(jnp.int32, (modes, groups), 1)
    amplitude = res_ref[...] * jnp.sqrt(one_minus_exp(2.0 * rate_ref[...]) * (1.0 / modes))
    lag_sums[...] = jnp.zeros_like(lag_sums)

    def convolve(index, carry):
        rates = rolled(rate_ref[...], index)
        amps = rolled(amplitude, index)
        tails = []
        weights = []
        sums = lag_sums[...]
        for part in range(tile // half):
            where_half = lanes(index * (tile // half) + part, half)
            grads = grad_ref[:, where_half]
            ins = dot(reverse, in_ref[:, where_half]).astype(BF16)
            doubled = jnp.concatenate([grads, grads], axis=0)
            result = jnp.zeros((rows, half), F32)
            for g8 in range(half_groups):
                g = part * half_groups + g8
                rate = rates[:, g : g + 1]
                amp = amps[:, g : g + 1]
                decays = decay[pl.ds(pl.multiple_of(index * stacked + g * modes, modes), modes), :]
                filt = jnp.sum(amp * decays, axis=0, keepdims=True)
                shifted = pltpu.roll(
                    jnp.broadcast_to(filt, (rows, rows)), 0, 1, stride=1, stride_axis=0
                )
                high, low = split(jnp.where(causal, shifted, 0.0))
                wide = dot(jnp.concatenate([high, low], axis=1), doubled)
                result = jnp.where(half_lane_group == g8, wide, result)
                masked = jnp.where(half_lane_group == g8, ins, jnp.zeros_like(ins))
                products = lax.dot_general(
                    masked, grads, (((1,), (1,)), ((), ())), preferred_element_type=F32
                )
                skewed = pltpu.roll(products, 1, 1, stride=1, stride_axis=0)
                lagged = jnp.sum(jnp.where(inside, skewed, 0.0), axis=0, keepdims=True)
                value = jnp.sum(decays * lagged, axis=1, keepdims=True)
                sums = jnp.where(group_lane == index * tile_groups + g, value, sums)
                remaining = jnp.exp(-rate * behind)
                tails.append(remaining)
                weights.append(amp * remaining)
            out_ref[:, where_half] = result
        lag_sums[...] = sums
        high, low = split(jnp.concatenate(tails, axis=0))
        ins = in_ref[:, lanes(index, tile)]
        wide = dot(jnp.concatenate([high, low], axis=1), jnp.concatenate([ins, ins], axis=0))
        tail[:, lanes(index, tile)] = compress(wide)
        high, low = split(jnp.concatenate(weights, axis=0).T)
        tail_high[index] = high
        tail_low[index] = low

        @pl.when(lax.rem(index, per_step) == per_step - 1)
        def _():
            exchange(index // per_step)

        return carry

    lax.fori_loop(0, tiles, convolve, 0)
    for step in range(tiles // per_step, steps):
        exchange(step)

    def enter(index, sums):
        q, inner = index // chunk_tiles, lax.rem(index, chunk_tiles)
        entry = incoming[q, :, lanes(inner, tile)]
        power = decay_pow[q, :, lanes(inner, tile)]
        entry = jnp.where(upper == 0, pair[q, :, lanes(inner, tile)] + power * entry, entry)
        incoming[q, :, lanes(inner, tile)] = entry
        value = tail[:, lanes(index, tile)] * entry
        high = value.astype(BF16)
        rest = value - high.astype(F32)
        middle, low = split(rest)
        chan_group = lax.broadcasted_iota(jnp.int32, (tile, groups), 0) // per_group
        member = lax.broadcasted_iota(jnp.int32, (tile, groups), 1) == chan_group + index * tile_groups
        member = jnp.where(member, 1.0, 0.0).astype(BF16)
        found = dot(jnp.concatenate([high, middle, low], axis=0), member)
        return sums + found[:modes] + found[modes : 2 * modes] + found[2 * modes :]

    partial[...] = lax.fori_loop(0, tiles, enter, lag_sums[...])

    def seq_copy(offset):
        return pltpu.make_async_remote_copy(
            partial, from_seq.at[offset - 1], seq_send.at[offset - 1], seq_recv.at[offset - 1],
            device_id={"seq": lax.rem(my_seq + offset, seqs)}, device_id_type=MESH,
        )

    def ctx_copy(offset):
        return pltpu.make_async_remote_copy(
            seq_sum, from_ctx.at[offset - 1], ctx_send.at[offset - 1], ctx_recv.at[offset - 1],
            device_id={"ctx": lax.rem(me + offset, shards)}, device_id_type=MESH,
        )

    for offset in range(1, seqs):
        seq_copy(offset).start()

    def carry_in(index, carry):
        q, inner = index // chunk_tiles, lax.rem(index, chunk_tiles)
        entry = incoming[q, :, lanes(inner, tile)]
        blocks = jnp.concatenate(
            [jnp.where(lane_group == g, entry, 0.0) for g in range(tile_groups)], axis=0
        )
        high, low = split(blocks)
        left = tail_high[index]
        out_ref[:, lanes(index, tile)] += dot(
            jnp.concatenate([left, left, tail_low[index]], axis=1),
            jnp.concatenate([high, low, high], axis=0),
        )
        return carry

    lax.fori_loop(0, tiles // 2, carry_in, 0)
    for offset in range(1, seqs):
        seq_copy(offset).wait_recv()

    def ordered(mine, received, place_here, count):
        added = jnp.zeros((modes, groups), F32)
        for source in range(count):
            value = jnp.where(place_here == source, mine, 0.0)
            for offset in range(1, count):
                value = jnp.where(
                    lax.rem(source + offset, count) == place_here, received[offset - 1], value
                )
            added = added + value
        return added

    seq_sum[...] = ordered(partial[...], from_seq, my_seq, seqs)
    for offset in range(1, shards):
        ctx_copy(offset).start()
    lax.fori_loop(tiles // 2, tiles, carry_in, 0)
    for offset in range(1, shards):
        ctx_copy(offset).wait_recv()

    def gather_sum(source, added):
        offset = lax.rem(me - source + shards, shards)
        slot = jnp.maximum(offset - 1, 0)
        return added + jnp.where(offset == 0, seq_sum[...], from_ctx[slot])

    total = lax.fori_loop(0, shards, gather_sum, jnp.zeros((modes, groups), F32))
    scale = 1.0 / float(seqs * shards * rows * per_group)
    total_ref[...] = total * jnp.sqrt(one_minus_exp(2.0 * rate_ref[...]) * scale)

    for q in range(chunks):
        pair_copy(q).wait_send()
        if pairs > 1:
            @pl.when(place > 0)
            def _(q=q):
                chain_copy(q).wait_send()
    for offset in range(1, seqs):
        seq_copy(offset).wait_send()
    for offset in range(1, shards):
        ctx_copy(offset).wait_send()


def local(shards, seqs, grad_out, inputs, residues, rates):
    rows, width = grad_out.shape[1:]
    modes, groups = residues.shape
    chunks = 4
    tile = 256
    chunk_shape = (chunks, modes, width // chunks)
    small = (modes, groups)
    states = pltpu.VMEM(chunk_shape, F32)
    dma = pltpu.SemaphoreType.DMA
    vmem = pl.BlockSpec(memory_space=pltpu.VMEM)
    grad_in, total = pl.pallas_call(
        functools.partial(body, shards, seqs, chunks),
        out_shape=(
            jax.ShapeDtypeStruct((rows, width), F32),
            jax.ShapeDtypeStruct(small, F32),
        ),
        in_specs=[vmem] * 4,
        out_specs=(vmem, vmem),
        scratch_shapes=[
            states, states, states, states, states, states,
            pltpu.VMEM((groups * modes, rows), F32),
            pltpu.VMEM((width // tile, rows, tile // (width // groups) * modes), BF16),
            pltpu.VMEM((width // tile, rows, tile // (width // groups) * modes), BF16),
            pltpu.VMEM((modes, width), F32),
            pltpu.VMEM(small, F32),
            pltpu.VMEM(small, F32),
            pltpu.VMEM((seqs - 1,) + small, F32),
            pltpu.VMEM(small, F32),
            pltpu.VMEM((shards - 1,) + small, F32),
            dma((chunks,)), dma((chunks,)), dma((chunks,)), dma((chunks,)),
            dma((seqs - 1,)), dma((seqs - 1,)), dma((shards - 1,)), dma((shards - 1,)),
        ],
        compiler_params=pltpu.CompilerParams(
            collective_id=0, has_side_effects=True, vmem_limit_bytes=40 * 1024 * 1024
        ),
    )(grad_out[0], inputs[0], residues, rates)
    return grad_in[None], total


def solution(mesh):
    placed = (P("seq", "ctx", None), P("seq", "ctx", None), P(), P())
    return jax.shard_map(
        functools.partial(local, mesh.shape["ctx"], mesh.shape["seq"]),
        mesh=mesh, in_specs=placed, out_specs=(P("seq", "ctx", None), P()), check_vma=False,
    )
```

```python
import functools

import jax
import jax.numpy as jnp
from jax import lax
from jax.experimental import pallas as pl
from jax.experimental.pallas import tpu as pltpu
from jax.sharding import PartitionSpec as P

MESH = pl.DeviceIdType.MESH
F32 = jnp.float32
BF16 = jnp.bfloat16


def dot(a, b):
    return jnp.dot(a, b, preferred_element_type=F32)


def split(a):
    high = a.astype(BF16)
    return high, (a - high.astype(F32)).astype(BF16)


def one_minus_exp(u):
    series = 1.0 - u * (1.0 / 8.0)
    for order in (7.0, 6.0, 5.0, 4.0, 3.0, 2.0):
        series = 1.0 - u * (1.0 / order) * series
    return u * series


def body(
    shards, seqs, chunks, grad_hbm, in_hbm, res_hbm, rate_hbm, out_ref, total_ref,
    grad_ref, in_ref, res_ref, rate_ref, small_sem, grad_sem, in_sem,
    own, pair, joined, incoming, outgoing, decay_pow, decay, tail_high, tail_low, tail, lag_sums,
    partial, from_seq, seq_sum, from_ctx,
    pair_send, pair_recv, chain_send, chain_recv, seq_send, seq_recv, ctx_send, ctx_recv,
):
    rows, width = grad_ref.shape
    modes, groups = res_ref.shape
    per_group = width // groups
    tile_groups = modes if modes * per_group == 256 else 256 // per_group
    tile = tile_groups * per_group
    tiles = width // tile
    chunk_tiles = tiles // chunks
    half = 128
    half_groups = half // per_group
    stacked = tile_groups * modes
    pairs = shards // 2

    span = width // chunks
    rate_copy = pltpu.make_async_copy(rate_hbm, rate_ref, small_sem.at[0])
    res_copy = pltpu.make_async_copy(res_hbm, res_ref, small_sem.at[1])
    in_copy = pltpu.make_async_copy(in_hbm, in_ref, in_sem)
    grad_copies = [
        pltpu.make_async_copy(
            grad_hbm.at[:, q * span : (q + 1) * span],
            grad_ref.at[:, q * span : (q + 1) * span],
            grad_sem.at[q],
        )
        for q in range(chunks)
    ]
    rate_copy.start()
    for copy in grad_copies:
        copy.start()
    in_copy.start()
    res_copy.start()

    me = lax.axis_index("ctx")
    my_seq = lax.axis_index("seq")
    upper = me % 2
    place = me // 2
    partner = me + 1 - 2 * upper
    hops = pairs - 1 - place

    barrier = pltpu.get_barrier_semaphore()
    for offset in range(1, shards):
        pl.semaphore_signal(
            barrier, inc=1, device_id={"ctx": lax.rem(me + offset, shards)}, device_id_type=MESH
        )
    for offset in range(1, seqs):
        pl.semaphore_signal(
            barrier, inc=1, device_id={"seq": lax.rem(my_seq + offset, seqs)}, device_id_type=MESH
        )

    lane_group = lax.broadcasted_iota(jnp.int32, (modes, tile), 1) // per_group
    ahead = lax.broadcasted_iota(jnp.int32, (modes, rows), 1).astype(F32)
    behind = float(rows) - ahead

    def rolled(values, index):
        return pltpu.roll(values, lax.rem(groups - index * tile_groups, groups), 1)

    def compress(wide):
        kept = jnp.zeros((modes, tile), F32)
        for g in range(tile_groups):
            kept = jnp.where(lane_group == g, wide[g * modes : (g + 1) * modes, :], kept)
        return kept

    def lanes(index, size):
        return pl.ds(pl.multiple_of(index * size, size), size)

    def pair_copy(q):
        return pltpu.make_async_remote_copy(
            own.at[q], pair.at[q], pair_send.at[q], pair_recv.at[q],
            device_id={"ctx": partner}, device_id_type=MESH,
        )

    def chain_copy(q):
        return pltpu.make_async_remote_copy(
            outgoing.at[q], incoming.at[q], chain_send.at[q], chain_recv.at[q],
            device_id={"ctx": lax.rem(me + shards - 2, shards)}, device_id_type=MESH,
        )

    rate_copy.wait()
    for q in range(chunks):
        grad_copies[q].wait()

        def summarize(step, carry, q=q):
            index = q * chunk_tiles + step
            rates = rolled(rate_ref[...], index)
            spread = jnp.zeros((modes, tile), F32)
            parts = []
            for g in range(tile_groups):
                rate = rates[:, g : g + 1]
                parts.append(jnp.exp(-rate * ahead))
                spread = jnp.where(lane_group == g, rate, spread)
            decays = jnp.concatenate(parts, axis=0)
            decay[lanes(index, stacked), :] = decays
            high, low = split(decays)
            grads = grad_ref[:, lanes(index, tile)]
            wide = dot(jnp.concatenate([high, low], axis=1), jnp.concatenate([grads, grads], axis=0))
            own[q, :, lanes(step, tile)] = compress(wide)
            decay_pow[q, :, lanes(step, tile)] = jnp.exp(-float(rows) * spread)
            return carry

        lax.fori_loop(0, chunk_tiles, summarize, 0)
        if q == 0:
            pl.semaphore_wait(barrier, shards - 1 + seqs - 1)
        pair_copy(q).start()

    in_copy.wait()
    res_copy.wait()

    def exchange(step):
        @pl.when(step < chunks)
        def _():
            pair_copy(step).wait_recv()
            power = decay_pow[step]
            mine, other = own[step], pair[step]
            near = jnp.where(upper == 0, mine, other)
            far = jnp.where(upper == 0, other, mine)
            joined[step] = near + power * far

            @pl.when(hops == 0)
            def _():
                incoming[step] = jnp.zeros(incoming.shape[1:], F32)
                if pairs > 1:
                    outgoing[step] = joined[step]
                    chain_copy(step).start()

        if pairs > 1:
            q = step - hops

            @pl.when((hops > 0) & (q >= 0) & (q < chunks))
            def _():
                chain_copy(q).wait_recv()

                @pl.when(place > 0)
                def _():
                    power = decay_pow[q]
                    outgoing[q] = joined[q] + power * power * incoming[q]
                    chain_copy(q).start()

    steps = chunks + pairs - 1
    per_step = max(1, tiles // steps)

    sub = min(32, rows)
    subs = rows // sub
    sub_lane_group = lax.broadcasted_iota(jnp.int32, (sub, half), 1) // per_group
    folded_group = lax.rem(
        lax.broadcasted_iota(jnp.int32, (sub, subs * half), 1), half
    ) // per_group
    row_of = lax.broadcasted_iota(jnp.int32, (rows, rows), 0)
    col_of = lax.broadcasted_iota(jnp.int32, (rows, rows), 1)
    sub_row = lax.broadcasted_iota(jnp.int32, (sub, rows), 0)
    sub_col = lax.broadcasted_iota(jnp.int32, (sub, rows), 1)
    causal = sub_col >= sub_row
    inside = sub_col <= rows - sub + sub_row
    mirrored = (row_of // sub == col_of // sub) & (
        lax.rem(row_of, sub) + lax.rem(col_of, sub) == sub - 1
    )
    reverse = jnp.where(mirrored, 1.0, 0.0).astype(BF16)
    group_lane = lax.broadcasted_iota(jnp.int32, (modes, groups), 1)
    amplitude = res_ref[...] * jnp.sqrt(one_minus_exp(2.0 * rate_ref[...]) * (1.0 / modes))
    lag_sums[...] = jnp.zeros_like(lag_sums)

    def convolve(index, carry):
        rates = rolled(rate_ref[...], index)
        amps = rolled(amplitude, index)
        tails = []
        weights = []
        sums = lag_sums[...]
        for part in range(tile // half):
            where_half = lanes(index * (tile // half) + part, half)
            grads = grad_ref[:, where_half]
            ins = dot(reverse, in_ref[:, where_half]).astype(BF16)
            shifted = jnp.concatenate(
                [grads]
                + [
                    jnp.concatenate(
                        [grads[r * sub :], jnp.zeros((r * sub, half), BF16)], axis=0
                    )
                    for r in range(1, subs)
                ],
                axis=1,
            )
            folded = jnp.concatenate([ins[r * sub : (r + 1) * sub] for r in range(subs)], axis=1)
            filters, masked, kept = [], [], []
            for g8 in range(half_groups):
                g = part * half_groups + g8
                rate = rates[:, g : g + 1]
                amp = amps[:, g : g + 1]
                decays = decay[pl.ds(pl.multiple_of(index * stacked + g * modes, modes), modes), :]
                kept.append(decays)
                filt = jnp.sum(amp * decays, axis=0, keepdims=True)
                toeplitz = pltpu.roll(
                    jnp.broadcast_to(filt, (sub, rows)), 0, 1, stride=1, stride_axis=0
                )
                high, low = split(jnp.where(causal, toeplitz, 0.0))
                filters.append(jnp.concatenate([high, low], axis=1))
                masked.append(jnp.where(folded_group == g8, folded, jnp.zeros_like(folded)))
                remaining = jnp.exp(-rate * behind)
                tails.append(remaining)
                weights.append(amp * remaining)
            wide = dot(jnp.concatenate(filters, axis=0), jnp.concatenate([shifted, shifted], axis=0))
            for r in range(subs):
                result = jnp.zeros((sub, half), F32)
                for g8 in range(half_groups):
                    piece = wide[g8 * sub : (g8 + 1) * sub, r * half : (r + 1) * half]
                    result = jnp.where(sub_lane_group == g8, piece, result)
                out_ref[r * sub : (r + 1) * sub, where_half] = result
            products = lax.dot_general(
                jnp.concatenate(masked, axis=0), shifted, (((1,), (1,)), ((), ())),
                preferred_element_type=F32,
            )
            for g8 in range(half_groups):
                g = part * half_groups + g8
                skewed = pltpu.roll(
                    products[g8 * sub : (g8 + 1) * sub], rows + 1 - sub, 1, stride=1, stride_axis=0
                )
                lagged = jnp.sum(jnp.where(inside, skewed, 0.0), axis=0, keepdims=True)
                value = jnp.sum(kept[g8] * lagged, axis=1, keepdims=True)
                sums = jnp.where(group_lane == index * tile_groups + g, value, sums)
        lag_sums[...] = sums
        high, low = split(jnp.concatenate(tails, axis=0))
        ins = in_ref[:, lanes(index, tile)]
        wide = dot(jnp.concatenate([high, low], axis=1), jnp.concatenate([ins, ins], axis=0))
        tail[:, lanes(index, tile)] = compress(wide)
        high, low = split(jnp.concatenate(weights, axis=0).T)
        tail_high[index] = high
        tail_low[index] = low

        @pl.when(lax.rem(index, per_step) == per_step - 1)
        def _():
            exchange(index // per_step)

        return carry

    lax.fori_loop(0, tiles, convolve, 0)
    for step in range(tiles // per_step, steps):
        exchange(step)

    def enter(index, sums):
        q, inner = index // chunk_tiles, lax.rem(index, chunk_tiles)
        entry = incoming[q, :, lanes(inner, tile)]
        power = decay_pow[q, :, lanes(inner, tile)]
        entry = jnp.where(upper == 0, pair[q, :, lanes(inner, tile)] + power * entry, entry)
        incoming[q, :, lanes(inner, tile)] = entry
        value = tail[:, lanes(index, tile)] * entry
        high = value.astype(BF16)
        rest = value - high.astype(F32)
        middle, low = split(rest)
        chan_group = lax.broadcasted_iota(jnp.int32, (tile, groups), 0) // per_group
        member = lax.broadcasted_iota(jnp.int32, (tile, groups), 1) == chan_group + index * tile_groups
        member = jnp.where(member, 1.0, 0.0).astype(BF16)
        found = dot(jnp.concatenate([high, middle, low], axis=0), member)
        return sums + found[:modes] + found[modes : 2 * modes] + found[2 * modes :]

    partial[...] = lax.fori_loop(0, tiles, enter, lag_sums[...])

    def seq_copy(offset):
        return pltpu.make_async_remote_copy(
            partial, from_seq.at[offset - 1], seq_send.at[offset - 1], seq_recv.at[offset - 1],
            device_id={"seq": lax.rem(my_seq + offset, seqs)}, device_id_type=MESH,
        )

    def ctx_copy(offset):
        return pltpu.make_async_remote_copy(
            seq_sum, from_ctx.at[offset - 1], ctx_send.at[offset - 1], ctx_recv.at[offset - 1],
            device_id={"ctx": lax.rem(me + offset, shards)}, device_id_type=MESH,
        )

    for offset in range(1, seqs):
        seq_copy(offset).start()

    def carry_in(index, carry):
        q, inner = index // chunk_tiles, lax.rem(index, chunk_tiles)
        entry = incoming[q, :, lanes(inner, tile)]
        high, low = split(entry)

        def blocks(value):
            return jnp.concatenate(
                [jnp.where(lane_group == g, value, jnp.zeros_like(value)) for g in range(tile_groups)],
                axis=0,
            )

        left = tail_high[index]
        both = dot(jnp.concatenate([left, tail_low[index]], axis=0), blocks(high))
        rest = dot(left, blocks(low))
        out_ref[:, lanes(index, tile)] += both[:rows] + both[rows:] + rest
        return carry

    lax.fori_loop(0, tiles // 2, carry_in, 0)
    for offset in range(1, seqs):
        seq_copy(offset).wait_recv()

    def ordered(mine, received, place_here, count):
        added = jnp.zeros((modes, groups), F32)
        for source in range(count):
            value = jnp.where(place_here == source, mine, 0.0)
            for offset in range(1, count):
                value = jnp.where(
                    lax.rem(source + offset, count) == place_here, received[offset - 1], value
                )
            added = added + value
        return added

    seq_sum[...] = ordered(partial[...], from_seq, my_seq, seqs)
    for offset in range(1, shards):
        ctx_copy(offset).start()
    lax.fori_loop(tiles // 2, tiles, carry_in, 0)
    for offset in range(1, shards):
        ctx_copy(offset).wait_recv()

    def gather_sum(source, added):
        offset = lax.rem(me - source + shards, shards)
        slot = jnp.maximum(offset - 1, 0)
        return added + jnp.where(offset == 0, seq_sum[...], from_ctx[slot])

    total = lax.fori_loop(0, shards, gather_sum, jnp.zeros((modes, groups), F32))
    scale = 1.0 / float(seqs * shards * rows * per_group)
    total_ref[...] = total * jnp.sqrt(one_minus_exp(2.0 * rate_ref[...]) * scale)

    for q in range(chunks):
        pair_copy(q).wait_send()
        if pairs > 1:
            @pl.when(place > 0)
            def _(q=q):
                chain_copy(q).wait_send()
    for offset in range(1, seqs):
        seq_copy(offset).wait_send()
    for offset in range(1, shards):
        ctx_copy(offset).wait_send()


def local(shards, seqs, grad_out, inputs, residues, rates):
    rows, width = grad_out.shape[1:]
    modes, groups = residues.shape
    chunks = 4
    tile = 256
    chunk_shape = (chunks, modes, width // chunks)
    small = (modes, groups)
    states = pltpu.VMEM(chunk_shape, F32)
    dma = pltpu.SemaphoreType.DMA
    vmem = pl.BlockSpec(memory_space=pltpu.VMEM)
    grad_in, total = pl.pallas_call(
        functools.partial(body, shards, seqs, chunks),
        out_shape=(
            jax.ShapeDtypeStruct((rows, width), F32),
            jax.ShapeDtypeStruct(small, F32),
        ),
        in_specs=[pl.BlockSpec(memory_space=pltpu.HBM)] * 4,
        out_specs=(vmem, vmem),
        scratch_shapes=[
            pltpu.VMEM((rows, width), BF16), pltpu.VMEM((rows, width), BF16),
            pltpu.VMEM(small, F32), pltpu.VMEM(small, F32), dma((2,)), dma((chunks,)), dma,
            states, states, states, states, states, states,
            pltpu.VMEM((groups * modes, rows), F32),
            pltpu.VMEM((width // tile, rows, tile // (width // groups) * modes), BF16),
            pltpu.VMEM((width // tile, rows, tile // (width // groups) * modes), BF16),
            pltpu.VMEM((modes, width), F32),
            pltpu.VMEM(small, F32),
            pltpu.VMEM(small, F32),
            pltpu.VMEM((seqs - 1,) + small, F32),
            pltpu.VMEM(small, F32),
            pltpu.VMEM((shards - 1,) + small, F32),
            dma((chunks,)), dma((chunks,)), dma((chunks,)), dma((chunks,)),
            dma((seqs - 1,)), dma((seqs - 1,)), dma((shards - 1,)), dma((shards - 1,)),
        ],
        compiler_params=pltpu.CompilerParams(
            collective_id=0, has_side_effects=True, vmem_limit_bytes=40 * 1024 * 1024
        ),
    )(grad_out[0], inputs[0], residues, rates)
    return grad_in[None], total


def solution(mesh):
    placed = (P("seq", "ctx", None), P("seq", "ctx", None), P(), P())
    return jax.shard_map(
        functools.partial(local, mesh.shape["ctx"], mesh.shape["seq"]),
        mesh=mesh, in_specs=placed, out_specs=(P("seq", "ctx", None), P()), check_vma=False,
    )
```

```python
import functools

import jax
import jax.numpy as jnp
from jax import lax
from jax.experimental import pallas as pl
from jax.experimental.pallas import tpu as pltpu
from jax.sharding import PartitionSpec as P

MESH = pl.DeviceIdType.MESH
F32 = jnp.float32
BF16 = jnp.bfloat16


def dot(a, b):
    return jnp.dot(a, b, preferred_element_type=F32)


def split(a):
    high = a.astype(BF16)
    return high, (a - high.astype(F32)).astype(BF16)


def one_minus_exp(u):
    series = 1.0 - u * (1.0 / 8.0)
    for order in (7.0, 6.0, 5.0, 4.0, 3.0, 2.0):
        series = 1.0 - u * (1.0 / order) * series
    return u * series


def body(
    shards, seqs, chunks, grad_hbm, in_hbm, res_hbm, rate_hbm, out_hbm, total_ref,
    grad_ref, in_ref, res_ref, rate_ref, out_ref, small_sem, grad_sem, in_sem, out_sem,
    own, pair, joined, incoming, outgoing, decay_pow, decay, tail_high, tail_low, tail, lag_sums,
    partial, from_seq, seq_sum, from_ctx,
    pair_send, pair_recv, chain_send, chain_recv, seq_send, seq_recv, ctx_send, ctx_recv,
):
    rows, width = grad_ref.shape
    modes, groups = res_ref.shape
    per_group = width // groups
    tile_groups = modes if modes * per_group == 256 else 256 // per_group
    tile = tile_groups * per_group
    tiles = width // tile
    chunk_tiles = tiles // chunks
    half = 128
    half_groups = half // per_group
    stacked = tile_groups * modes
    pairs = shards // 2

    span = width // chunks
    rate_copy = pltpu.make_async_copy(rate_hbm, rate_ref, small_sem.at[0])
    res_copy = pltpu.make_async_copy(res_hbm, res_ref, small_sem.at[1])
    in_copy = pltpu.make_async_copy(in_hbm, in_ref, in_sem)
    grad_copies = [
        pltpu.make_async_copy(
            grad_hbm.at[:, q * span : (q + 1) * span],
            grad_ref.at[:, q * span : (q + 1) * span],
            grad_sem.at[q],
        )
        for q in range(chunks)
    ]
    rate_copy.start()
    for copy in grad_copies:
        copy.start()
    in_copy.start()
    res_copy.start()

    me = lax.axis_index("ctx")
    my_seq = lax.axis_index("seq")
    upper = me % 2
    place = me // 2
    partner = me + 1 - 2 * upper
    hops = pairs - 1 - place

    barrier = pltpu.get_barrier_semaphore()
    for offset in range(1, shards):
        pl.semaphore_signal(
            barrier, inc=1, device_id={"ctx": lax.rem(me + offset, shards)}, device_id_type=MESH
        )
    for offset in range(1, seqs):
        pl.semaphore_signal(
            barrier, inc=1, device_id={"seq": lax.rem(my_seq + offset, seqs)}, device_id_type=MESH
        )

    lane_group = lax.broadcasted_iota(jnp.int32, (modes, tile), 1) // per_group
    ahead = lax.broadcasted_iota(jnp.int32, (modes, rows), 1).astype(F32)
    behind = float(rows) - ahead

    def rolled(values, index):
        return pltpu.roll(values, lax.rem(groups - index * tile_groups, groups), 1)

    def compress(wide):
        kept = jnp.zeros((modes, tile), F32)
        for g in range(tile_groups):
            kept = jnp.where(lane_group == g, wide[g * modes : (g + 1) * modes, :], kept)
        return kept

    def lanes(index, size):
        return pl.ds(pl.multiple_of(index * size, size), size)

    def pair_copy(q):
        return pltpu.make_async_remote_copy(
            own.at[q], pair.at[q], pair_send.at[q], pair_recv.at[q],
            device_id={"ctx": partner}, device_id_type=MESH,
        )

    def chain_copy(q):
        return pltpu.make_async_remote_copy(
            outgoing.at[q], incoming.at[q], chain_send.at[q], chain_recv.at[q],
            device_id={"ctx": lax.rem(me + shards - 2, shards)}, device_id_type=MESH,
        )

    rate_copy.wait()
    for q in range(chunks):
        grad_copies[q].wait()

        def summarize(step, carry, q=q):
            index = q * chunk_tiles + step
            rates = rolled(rate_ref[...], index)
            spread = jnp.zeros((modes, tile), F32)
            parts = []
            for g in range(tile_groups):
                rate = rates[:, g : g + 1]
                parts.append(jnp.exp(-rate * ahead))
                spread = jnp.where(lane_group == g, rate, spread)
            decays = jnp.concatenate(parts, axis=0)
            decay[lanes(index, stacked), :] = decays
            high, low = split(decays)
            grads = grad_ref[:, lanes(index, tile)]
            wide = dot(jnp.concatenate([high, low], axis=1), jnp.concatenate([grads, grads], axis=0))
            own[q, :, lanes(step, tile)] = compress(wide)
            decay_pow[q, :, lanes(step, tile)] = jnp.exp(-float(rows) * spread)
            return carry

        lax.fori_loop(0, chunk_tiles, summarize, 0, unroll=True)
        if q == 0:
            pl.semaphore_wait(barrier, shards - 1 + seqs - 1)
        pair_copy(q).start()

    in_copy.wait()
    res_copy.wait()

    def exchange(step):
        @pl.when(step < chunks)
        def _():
            pair_copy(step).wait_recv()
            power = decay_pow[step]
            mine, other = own[step], pair[step]
            near = jnp.where(upper == 0, mine, other)
            far = jnp.where(upper == 0, other, mine)
            joined[step] = near + power * far

            @pl.when(hops == 0)
            def _():
                incoming[step] = jnp.zeros(incoming.shape[1:], F32)
                if pairs > 1:
                    outgoing[step] = joined[step]
                    chain_copy(step).start()

        if pairs > 1:
            q = step - hops

            @pl.when((hops > 0) & (q >= 0) & (q < chunks))
            def _():
                chain_copy(q).wait_recv()

                @pl.when(place > 0)
                def _():
                    power = decay_pow[q]
                    outgoing[q] = joined[q] + power * power * incoming[q]
                    chain_copy(q).start()

    steps = chunks + pairs - 1
    per_step = max(1, tiles // steps)

    sub = min(32, rows)
    subs = rows // sub
    sub_lane_group = lax.broadcasted_iota(jnp.int32, (sub, half), 1) // per_group
    folded_group = lax.rem(
        lax.broadcasted_iota(jnp.int32, (sub, subs * half), 1), half
    ) // per_group
    row_of = lax.broadcasted_iota(jnp.int32, (rows, rows), 0)
    col_of = lax.broadcasted_iota(jnp.int32, (rows, rows), 1)
    sub_row = lax.broadcasted_iota(jnp.int32, (sub, rows), 0)
    sub_col = lax.broadcasted_iota(jnp.int32, (sub, rows), 1)
    causal = sub_col >= sub_row
    inside = sub_col <= rows - sub + sub_row
    mirrored = (row_of // sub == col_of // sub) & (
        lax.rem(row_of, sub) + lax.rem(col_of, sub) == sub - 1
    )
    reverse = jnp.where(mirrored, 1.0, 0.0).astype(BF16)
    group_lane = lax.broadcasted_iota(jnp.int32, (modes, groups), 1)
    amplitude = res_ref[...] * jnp.sqrt(one_minus_exp(2.0 * rate_ref[...]) * (1.0 / modes))
    lag_sums[...] = jnp.zeros_like(lag_sums)

    def convolve(index, carry):
        rates = rolled(rate_ref[...], index)
        amps = rolled(amplitude, index)
        tails = []
        weights = []
        sums = lag_sums[...]
        for part in range(tile // half):
            where_half = lanes(index * (tile // half) + part, half)
            grads = grad_ref[:, where_half]
            ins = dot(reverse, in_ref[:, where_half]).astype(BF16)
            shifted = jnp.concatenate(
                [grads]
                + [
                    jnp.concatenate(
                        [grads[r * sub :], jnp.zeros((r * sub, half), BF16)], axis=0
                    )
                    for r in range(1, subs)
                ],
                axis=1,
            )
            folded = jnp.concatenate([ins[r * sub : (r + 1) * sub] for r in range(subs)], axis=1)
            filters, masked, kept = [], [], []
            for g8 in range(half_groups):
                g = part * half_groups + g8
                rate = rates[:, g : g + 1]
                amp = amps[:, g : g + 1]
                decays = decay[pl.ds(pl.multiple_of(index * stacked + g * modes, modes), modes), :]
                kept.append(decays)
                filt = jnp.sum(amp * decays, axis=0, keepdims=True)
                toeplitz = pltpu.roll(
                    jnp.broadcast_to(filt, (sub, rows)), 0, 1, stride=1, stride_axis=0
                )
                high, low = split(jnp.where(causal, toeplitz, 0.0))
                filters.append(jnp.concatenate([high, low], axis=1))
                masked.append(jnp.where(folded_group == g8, folded, jnp.zeros_like(folded)))
                remaining = jnp.exp(-rate * behind)
                tails.append(remaining)
                weights.append(amp * remaining)
            wide = dot(jnp.concatenate(filters, axis=0), jnp.concatenate([shifted, shifted], axis=0))
            for r in range(subs):
                result = jnp.zeros((sub, half), F32)
                for g8 in range(half_groups):
                    piece = wide[g8 * sub : (g8 + 1) * sub, r * half : (r + 1) * half]
                    result = jnp.where(sub_lane_group == g8, piece, result)
                out_ref[r * sub : (r + 1) * sub, where_half] = result
            products = lax.dot_general(
                jnp.concatenate(masked, axis=0), shifted, (((1,), (1,)), ((), ())),
                preferred_element_type=F32,
            )
            for g8 in range(half_groups):
                g = part * half_groups + g8
                skewed = pltpu.roll(
                    products[g8 * sub : (g8 + 1) * sub], rows + 1 - sub, 1, stride=1, stride_axis=0
                )
                lagged = jnp.sum(jnp.where(inside, skewed, 0.0), axis=0, keepdims=True)
                value = jnp.sum(kept[g8] * lagged, axis=1, keepdims=True)
                sums = jnp.where(group_lane == index * tile_groups + g, value, sums)
        lag_sums[...] = sums
        high, low = split(jnp.concatenate(tails, axis=0))
        ins = in_ref[:, lanes(index, tile)]
        wide = dot(jnp.concatenate([high, low], axis=1), jnp.concatenate([ins, ins], axis=0))
        tail[:, lanes(index, tile)] = compress(wide)
        high, low = split(jnp.concatenate(weights, axis=0).T)
        tail_high[index] = high
        tail_low[index] = low

        return carry

    def advance(step, carry):
        for inner in range(per_step):
            convolve(step * per_step + inner, 0)
        exchange(step)
        return carry

    lax.fori_loop(0, tiles // per_step, advance, 0)
    for index in range(tiles // per_step * per_step, tiles):
        convolve(index, 0)
    for step in range(tiles // per_step, steps):
        exchange(step)

    def enter(index, sums):
        q, inner = index // chunk_tiles, lax.rem(index, chunk_tiles)
        entry = incoming[q, :, lanes(inner, tile)]
        power = decay_pow[q, :, lanes(inner, tile)]
        entry = jnp.where(upper == 0, pair[q, :, lanes(inner, tile)] + power * entry, entry)
        incoming[q, :, lanes(inner, tile)] = entry
        value = tail[:, lanes(index, tile)] * entry
        high = value.astype(BF16)
        rest = value - high.astype(F32)
        middle, low = split(rest)
        chan_group = lax.broadcasted_iota(jnp.int32, (tile, groups), 0) // per_group
        member = lax.broadcasted_iota(jnp.int32, (tile, groups), 1) == chan_group + index * tile_groups
        member = jnp.where(member, 1.0, 0.0).astype(BF16)
        found = dot(jnp.concatenate([high, middle, low], axis=0), member)
        return sums + found[:modes] + found[modes : 2 * modes] + found[2 * modes :]

    partial[...] = lax.fori_loop(0, tiles, enter, lag_sums[...], unroll=4)

    def seq_copy(offset):
        return pltpu.make_async_remote_copy(
            partial, from_seq.at[offset - 1], seq_send.at[offset - 1], seq_recv.at[offset - 1],
            device_id={"seq": lax.rem(my_seq + offset, seqs)}, device_id_type=MESH,
        )

    def ctx_copy(offset):
        return pltpu.make_async_remote_copy(
            seq_sum, from_ctx.at[offset - 1], ctx_send.at[offset - 1], ctx_recv.at[offset - 1],
            device_id={"ctx": lax.rem(me + offset, shards)}, device_id_type=MESH,
        )

    for offset in range(1, seqs):
        seq_copy(offset).start()

    def carry_in(index, carry):
        q, inner = index // chunk_tiles, lax.rem(index, chunk_tiles)
        entry = incoming[q, :, lanes(inner, tile)]
        high, low = split(entry)

        def blocks(value):
            return jnp.concatenate(
                [jnp.where(lane_group == g, value, jnp.zeros_like(value)) for g in range(tile_groups)],
                axis=0,
            )

        left = tail_high[index]
        both = dot(jnp.concatenate([left, tail_low[index]], axis=0), blocks(high))
        rest = dot(left, blocks(low))
        out_ref[:, lanes(index, tile)] += both[:rows] + both[rows:] + rest
        return carry

    def out_copy(q):
        return pltpu.make_async_copy(
            out_ref.at[:, q * span : (q + 1) * span],
            out_hbm.at[:, q * span : (q + 1) * span],
            out_sem.at[q],
        )

    def finish(q):
        lax.fori_loop(q * chunk_tiles, (q + 1) * chunk_tiles, carry_in, 0, unroll=True)
        out_copy(q).start()

    for q in range(chunks // 2):
        finish(q)
    for offset in range(1, seqs):
        seq_copy(offset).wait_recv()

    def ordered(mine, received, place_here, count):
        added = jnp.zeros((modes, groups), F32)
        for source in range(count):
            value = jnp.where(place_here == source, mine, 0.0)
            for offset in range(1, count):
                value = jnp.where(
                    lax.rem(source + offset, count) == place_here, received[offset - 1], value
                )
            added = added + value
        return added

    seq_sum[...] = ordered(partial[...], from_seq, my_seq, seqs)
    for offset in range(1, shards):
        ctx_copy(offset).start()
    for q in range(chunks // 2, chunks):
        finish(q)
    for offset in range(1, shards):
        ctx_copy(offset).wait_recv()

    def gather_sum(source, added):
        offset = lax.rem(me - source + shards, shards)
        slot = jnp.maximum(offset - 1, 0)
        return added + jnp.where(offset == 0, seq_sum[...], from_ctx[slot])

    total = lax.fori_loop(0, shards, gather_sum, jnp.zeros((modes, groups), F32))
    scale = 1.0 / float(seqs * shards * rows * per_group)
    total_ref[...] = total * jnp.sqrt(one_minus_exp(2.0 * rate_ref[...]) * scale)

    for q in range(chunks):
        out_copy(q).wait()
        pair_copy(q).wait_send()
        if pairs > 1:
            @pl.when(place > 0)
            def _(q=q):
                chain_copy(q).wait_send()
    for offset in range(1, seqs):
        seq_copy(offset).wait_send()
    for offset in range(1, shards):
        ctx_copy(offset).wait_send()


def local(shards, seqs, grad_out, inputs, residues, rates):
    rows, width = grad_out.shape[1:]
    modes, groups = residues.shape
    chunks = 4
    tile = 256
    chunk_shape = (chunks, modes, width // chunks)
    small = (modes, groups)
    states = pltpu.VMEM(chunk_shape, F32)
    dma = pltpu.SemaphoreType.DMA
    vmem = pl.BlockSpec(memory_space=pltpu.VMEM)
    grad_in, total = pl.pallas_call(
        functools.partial(body, shards, seqs, chunks),
        out_shape=(
            jax.ShapeDtypeStruct((rows, width), F32),
            jax.ShapeDtypeStruct(small, F32),
        ),
        in_specs=[pl.BlockSpec(memory_space=pltpu.HBM)] * 4,
        out_specs=(pl.BlockSpec(memory_space=pltpu.HBM), vmem),
        scratch_shapes=[
            pltpu.VMEM((rows, width), BF16), pltpu.VMEM((rows, width), BF16),
            pltpu.VMEM(small, F32), pltpu.VMEM(small, F32), pltpu.VMEM((rows, width), F32),
            dma((2,)), dma((chunks,)), dma, dma((chunks,)),
            states, states, states, states, states, states,
            pltpu.VMEM((groups * modes, rows), F32),
            pltpu.VMEM((width // tile, rows, tile // (width // groups) * modes), BF16),
            pltpu.VMEM((width // tile, rows, tile // (width // groups) * modes), BF16),
            pltpu.VMEM((modes, width), F32),
            pltpu.VMEM(small, F32),
            pltpu.VMEM(small, F32),
            pltpu.VMEM((seqs - 1,) + small, F32),
            pltpu.VMEM(small, F32),
            pltpu.VMEM((shards - 1,) + small, F32),
            dma((chunks,)), dma((chunks,)), dma((chunks,)), dma((chunks,)),
            dma((seqs - 1,)), dma((seqs - 1,)), dma((shards - 1,)), dma((shards - 1,)),
        ],
        compiler_params=pltpu.CompilerParams(
            collective_id=0, has_side_effects=True, vmem_limit_bytes=63 * 1024 * 1024
        ),
    )(grad_out[0], inputs[0], residues, rates)
    return grad_in[None], total


def solution(mesh):
    placed = (P("seq", "ctx", None), P("seq", "ctx", None), P(), P())
    return jax.shard_map(
        functools.partial(local, mesh.shape["ctx"], mesh.shape["seq"]),
        mesh=mesh, in_specs=placed, out_specs=(P("seq", "ctx", None), P()), check_vma=False,
    )
```

```python
import functools

import jax
import jax.numpy as jnp
from jax import lax
from jax.experimental import pallas as pl
from jax.experimental.pallas import tpu as pltpu
from jax.sharding import PartitionSpec as P

MESH = pl.DeviceIdType.MESH
F32 = jnp.float32
BF16 = jnp.bfloat16


def dot(a, b):
    return jnp.dot(a, b, preferred_element_type=F32)


def split(a):
    high = a.astype(BF16)
    return high, (a - high.astype(F32)).astype(BF16)


def one_minus_exp(u):
    series = 1.0 - u * (1.0 / 8.0)
    for order in (7.0, 6.0, 5.0, 4.0, 3.0, 2.0):
        series = 1.0 - u * (1.0 / order) * series
    return u * series


def body(
    shards, seqs, chunks, grad_hbm, in_hbm, res_hbm, rate_hbm, out_hbm, total_ref,
    grad_ref, in_ref, res_ref, rate_ref, out_ref, small_sem, grad_sem, in_sem, out_sem,
    own, pair, joined, incoming, outgoing, decay_pow, decay, tail_high, tail_low, tail, lag_sums,
    partial, from_seq, seq_sum, from_ctx,
    pair_send, pair_recv, chain_send, chain_recv, seq_send, seq_recv, ctx_send, ctx_recv,
):
    rows, width = grad_ref.shape
    modes, groups = res_ref.shape
    per_group = width // groups
    tile_groups = modes if modes * per_group == 256 else 256 // per_group
    tile = tile_groups * per_group
    tiles = width // tile
    chunk_tiles = tiles // chunks
    half = 128
    half_groups = half // per_group
    stacked = tile_groups * modes
    pairs = shards // 2

    span = width // chunks
    rate_copy = pltpu.make_async_copy(rate_hbm, rate_ref, small_sem.at[0])
    res_copy = pltpu.make_async_copy(res_hbm, res_ref, small_sem.at[1])
    in_copy = pltpu.make_async_copy(in_hbm, in_ref, in_sem)
    grad_copies = [
        pltpu.make_async_copy(
            grad_hbm.at[:, q * span : (q + 1) * span],
            grad_ref.at[:, q * span : (q + 1) * span],
            grad_sem.at[q],
        )
        for q in range(chunks)
    ]
    rate_copy.start()
    for copy in grad_copies:
        copy.start()
    in_copy.start()
    res_copy.start()

    me = lax.axis_index("ctx")
    my_seq = lax.axis_index("seq")
    upper = me % 2
    place = me // 2
    partner = me + 1 - 2 * upper
    hops = pairs - 1 - place

    barrier = pltpu.get_barrier_semaphore()
    for offset in range(1, shards):
        pl.semaphore_signal(
            barrier, inc=1, device_id={"ctx": lax.rem(me + offset, shards)}, device_id_type=MESH
        )
    for offset in range(1, seqs):
        pl.semaphore_signal(
            barrier, inc=1, device_id={"seq": lax.rem(my_seq + offset, seqs)}, device_id_type=MESH
        )

    lane_group = lax.broadcasted_iota(jnp.int32, (modes, tile), 1) // per_group
    ahead = lax.broadcasted_iota(jnp.int32, (modes, rows), 1).astype(F32)
    behind = float(rows) - ahead

    def rolled(values, index):
        return pltpu.roll(values, lax.rem(groups - index * tile_groups, groups), 1)

    def compress(wide):
        kept = jnp.zeros((modes, tile), F32)
        for g in range(tile_groups):
            kept = jnp.where(lane_group == g, wide[g * modes : (g + 1) * modes, :], kept)
        return kept

    def lanes(index, size):
        return pl.ds(pl.multiple_of(index * size, size), size)

    def pair_copy(q):
        return pltpu.make_async_remote_copy(
            own.at[q], pair.at[q], pair_send.at[q], pair_recv.at[q],
            device_id={"ctx": partner}, device_id_type=MESH,
        )

    def chain_copy(q):
        return pltpu.make_async_remote_copy(
            outgoing.at[q], incoming.at[q], chain_send.at[q], chain_recv.at[q],
            device_id={"ctx": lax.rem(me + shards - 2, shards)}, device_id_type=MESH,
        )

    rate_copy.wait()
    for q in range(chunks):
        grad_copies[q].wait()

        def summarize(step, carry, q=q):
            index = q * chunk_tiles + step
            rates = rolled(rate_ref[...], index)
            spread = jnp.zeros((modes, tile), F32)
            parts = []
            for g in range(tile_groups):
                rate = rates[:, g : g + 1]
                parts.append(jnp.exp(-rate * ahead))
                spread = jnp.where(lane_group == g, rate, spread)
            decays = jnp.concatenate(parts, axis=0)
            decay[lanes(index, stacked), :] = decays
            high, low = split(decays)
            grads = grad_ref[:, lanes(index, tile)]
            wide = dot(jnp.concatenate([high, low], axis=1), jnp.concatenate([grads, grads], axis=0))
            own[q, :, lanes(step, tile)] = compress(wide)
            decay_pow[q, :, lanes(step, tile)] = jnp.exp(-float(rows) * spread)
            return carry

        lax.fori_loop(0, chunk_tiles, summarize, 0, unroll=True)
        if q == 0:
            pl.semaphore_wait(barrier, shards - 1 + seqs - 1)
        pair_copy(q).start()

    in_copy.wait()
    res_copy.wait()

    def exchange(step):
        @pl.when(step < chunks)
        def _():
            pair_copy(step).wait_recv()
            power = decay_pow[step]
            mine, other = own[step], pair[step]
            near = jnp.where(upper == 0, mine, other)
            far = jnp.where(upper == 0, other, mine)
            joined[step] = near + power * far

            @pl.when(hops == 0)
            def _():
                incoming[step] = jnp.zeros(incoming.shape[1:], F32)
                if pairs > 1:
                    outgoing[step] = joined[step]
                    chain_copy(step).start()

        if pairs > 1:
            q = step - hops

            @pl.when((hops > 0) & (q >= 0) & (q < chunks))
            def _():
                chain_copy(q).wait_recv()

                @pl.when(place > 0)
                def _():
                    power = decay_pow[q]
                    outgoing[q] = joined[q] + power * power * incoming[q]
                    chain_copy(q).start()

    steps = chunks + pairs - 1
    per_step = max(1, tiles // steps)

    sub = min(32, rows)
    subs = rows // sub
    sub_lane_group = lax.broadcasted_iota(jnp.int32, (sub, half), 1) // per_group
    folded_masks = []
    for g in range(half_groups):
        mask = jnp.where(sub_lane_group == g, 1.0, 0.0).astype(BF16)
        folded_masks.append(jnp.concatenate([mask] * subs, axis=1))
    tile_masks = [jnp.where(lane_group == g, 1.0, 0.0).astype(BF16) for g in range(tile_groups)]
    row_of = lax.broadcasted_iota(jnp.int32, (rows, rows), 0)
    col_of = lax.broadcasted_iota(jnp.int32, (rows, rows), 1)
    sub_row = lax.broadcasted_iota(jnp.int32, (sub, rows), 0)
    sub_col = lax.broadcasted_iota(jnp.int32, (sub, rows), 1)
    causal = sub_col >= sub_row
    inside = sub_col <= rows - sub + sub_row
    mirrored = (row_of // sub == col_of // sub) & (
        lax.rem(row_of, sub) + lax.rem(col_of, sub) == sub - 1
    )
    reverse = jnp.where(mirrored, 1.0, 0.0).astype(BF16)
    group_lane = lax.broadcasted_iota(jnp.int32, (modes, groups), 1)
    amplitude = res_ref[...] * jnp.sqrt(one_minus_exp(2.0 * rate_ref[...]) * (1.0 / modes))
    lag_sums[...] = jnp.zeros_like(lag_sums)

    def folded_rows(grads):
        return jnp.concatenate(
            [grads]
            + [
                jnp.concatenate([grads[r * sub :], jnp.zeros((r * sub, half), BF16)], axis=0)
                for r in range(1, subs)
            ],
            axis=1,
        )

    def group_decays(index, g):
        return decay[pl.ds(pl.multiple_of(index * stacked + g * modes, modes), modes), :]

    def correlate(index):
        rates = rolled(rate_ref[...], index)
        amps = rolled(amplitude, index)
        tails = []
        weights = []
        sums = lag_sums[...]
        for part in range(tile // half):
            where_half = lanes(index * (tile // half) + part, half)
            shifted = folded_rows(grad_ref[:, where_half])
            ins = dot(reverse, in_ref[:, where_half]).astype(BF16)
            folded = jnp.concatenate([ins[r * sub : (r + 1) * sub] for r in range(subs)], axis=1)
            products = lax.dot_general(
                jnp.concatenate([folded * mask for mask in folded_masks], axis=0),
                shifted, (((1,), (1,)), ((), ())), preferred_element_type=F32,
            )
            for g8 in range(half_groups):
                g = part * half_groups + g8
                skewed = pltpu.roll(
                    products[g8 * sub : (g8 + 1) * sub], rows + 1 - sub, 1, stride=1, stride_axis=0
                )
                lagged = jnp.sum(jnp.where(inside, skewed, 0.0), axis=0, keepdims=True)
                value = jnp.sum(group_decays(index, g) * lagged, axis=1, keepdims=True)
                sums = jnp.where(group_lane == index * tile_groups + g, value, sums)
                remaining = jnp.exp(-rates[:, g : g + 1] * behind)
                tails.append(remaining)
                weights.append(amps[:, g : g + 1] * remaining)
        lag_sums[...] = sums
        high, low = split(jnp.concatenate(tails, axis=0))
        ins = in_ref[:, lanes(index, tile)]
        wide = dot(jnp.concatenate([high, low], axis=1), jnp.concatenate([ins, ins], axis=0))
        tail[:, lanes(index, tile)] = compress(wide)
        high, low = split(jnp.concatenate(weights, axis=0).T)
        tail_high[index] = high
        tail_low[index] = low

    def convolve(index):
        q, inner = index // chunk_tiles, lax.rem(index, chunk_tiles)
        amps = rolled(amplitude, index)
        high, low = split(incoming[q, :, lanes(inner, tile)])
        left = tail_high[index]
        both = dot(
            jnp.concatenate([left, tail_low[index]], axis=0),
            jnp.concatenate([high * mask for mask in tile_masks], axis=0),
        )
        rest = dot(left, jnp.concatenate([low * mask for mask in tile_masks], axis=0))
        entered = both[:rows] + both[rows:] + rest
        for part in range(tile // half):
            where_half = lanes(index * (tile // half) + part, half)
            shifted = folded_rows(grad_ref[:, where_half])
            filters = []
            for g8 in range(half_groups):
                g = part * half_groups + g8
                filt = jnp.sum(amps[:, g : g + 1] * group_decays(index, g), axis=0, keepdims=True)
                toeplitz = pltpu.roll(
                    jnp.broadcast_to(filt, (sub, rows)), 0, 1, stride=1, stride_axis=0
                )
                high, low = split(jnp.where(causal, toeplitz, 0.0))
                filters.append(jnp.concatenate([high, low], axis=1))
            wide = dot(jnp.concatenate(filters, axis=0), jnp.concatenate([shifted, shifted], axis=0))
            for r in range(subs):
                result = wide[:sub, r * half : (r + 1) * half]
                for g8 in range(1, half_groups):
                    piece = wide[g8 * sub : (g8 + 1) * sub, r * half : (r + 1) * half]
                    result = jnp.where(sub_lane_group == g8, piece, result)
                out_ref[r * sub : (r + 1) * sub, where_half] = (
                    result + entered[r * sub : (r + 1) * sub, part * half : (part + 1) * half]
                )

    def advance(step, carry):
        for inner in range(per_step):
            correlate(step * per_step + inner)
        exchange(step)
        return carry

    lax.fori_loop(0, tiles // per_step, advance, 0)
    for index in range(tiles // per_step * per_step, tiles):
        correlate(index)
    for step in range(tiles // per_step, steps):
        exchange(step)

    def enter(index, sums):
        q, inner = index // chunk_tiles, lax.rem(index, chunk_tiles)
        entry = incoming[q, :, lanes(inner, tile)]
        power = decay_pow[q, :, lanes(inner, tile)]
        entry = jnp.where(upper == 0, pair[q, :, lanes(inner, tile)] + power * entry, entry)
        incoming[q, :, lanes(inner, tile)] = entry
        value = tail[:, lanes(index, tile)] * entry
        high = value.astype(BF16)
        rest = value - high.astype(F32)
        middle, low = split(rest)
        chan_group = lax.broadcasted_iota(jnp.int32, (tile, groups), 0) // per_group
        member = lax.broadcasted_iota(jnp.int32, (tile, groups), 1) == chan_group + index * tile_groups
        member = jnp.where(member, 1.0, 0.0).astype(BF16)
        found = dot(jnp.concatenate([high, middle, low], axis=0), member)
        return sums + found[:modes] + found[modes : 2 * modes] + found[2 * modes :]

    partial[...] = lax.fori_loop(0, tiles, enter, lag_sums[...], unroll=4)

    def seq_copy(offset):
        return pltpu.make_async_remote_copy(
            partial, from_seq.at[offset - 1], seq_send.at[offset - 1], seq_recv.at[offset - 1],
            device_id={"seq": lax.rem(my_seq + offset, seqs)}, device_id_type=MESH,
        )

    def ctx_copy(offset):
        return pltpu.make_async_remote_copy(
            seq_sum, from_ctx.at[offset - 1], ctx_send.at[offset - 1], ctx_recv.at[offset - 1],
            device_id={"ctx": lax.rem(me + offset, shards)}, device_id_type=MESH,
        )

    for offset in range(1, seqs):
        seq_copy(offset).start()

    def out_copy(q):
        return pltpu.make_async_copy(
            out_ref.at[:, q * span : (q + 1) * span],
            out_hbm.at[:, q * span : (q + 1) * span],
            out_sem.at[q],
        )

    unrolled = 2 if chunk_tiles % 2 == 0 else 1

    def finish(q):
        def pieces(step, carry):
            for inner in range(unrolled):
                convolve(q * chunk_tiles + step * unrolled + inner)
            return carry

        lax.fori_loop(0, chunk_tiles // unrolled, pieces, 0)
        out_copy(q).start()

    for q in range(chunks // 2):
        finish(q)
    for offset in range(1, seqs):
        seq_copy(offset).wait_recv()

    def ordered(mine, received, place_here, count):
        added = jnp.zeros((modes, groups), F32)
        for source in range(count):
            value = jnp.where(place_here == source, mine, 0.0)
            for offset in range(1, count):
                value = jnp.where(
                    lax.rem(source + offset, count) == place_here, received[offset - 1], value
                )
            added = added + value
        return added

    seq_sum[...] = ordered(partial[...], from_seq, my_seq, seqs)
    for offset in range(1, shards):
        ctx_copy(offset).start()
    for q in range(chunks // 2, chunks):
        finish(q)
    for offset in range(1, shards):
        ctx_copy(offset).wait_recv()

    def gather_sum(source, added):
        offset = lax.rem(me - source + shards, shards)
        slot = jnp.maximum(offset - 1, 0)
        return added + jnp.where(offset == 0, seq_sum[...], from_ctx[slot])

    total = lax.fori_loop(0, shards, gather_sum, jnp.zeros((modes, groups), F32))
    total_ref[...] = total

    for q in range(chunks):
        out_copy(q).wait()
        pair_copy(q).wait_send()
        if pairs > 1:
            @pl.when(place > 0)
            def _(q=q):
                chain_copy(q).wait_send()
    for offset in range(1, seqs):
        seq_copy(offset).wait_send()
    for offset in range(1, shards):
        ctx_copy(offset).wait_send()


def write(count, grad_ref, sum_ref, rate_ref, out_ref, total_ref):
    out_ref[...] = grad_ref[...]
    total_ref[...] = sum_ref[...] * jnp.sqrt(one_minus_exp(2.0 * rate_ref[...]) * (1.0 / count))


def local(shards, seqs, grad_out, inputs, residues, rates):
    rows, width = grad_out.shape[1:]
    modes, groups = residues.shape
    chunks = 4
    tile = 256
    chunk_shape = (chunks, modes, width // chunks)
    small = (modes, groups)
    states = pltpu.VMEM(chunk_shape, F32)
    dma = pltpu.SemaphoreType.DMA
    vmem = pl.BlockSpec(memory_space=pltpu.VMEM)
    grad_in, total = pl.pallas_call(
        functools.partial(body, shards, seqs, chunks),
        out_shape=(
            jax.ShapeDtypeStruct((rows, width), F32),
            jax.ShapeDtypeStruct(small, F32),
        ),
        in_specs=[pl.BlockSpec(memory_space=pltpu.HBM)] * 4,
        out_specs=(pl.BlockSpec(memory_space=pltpu.HBM), vmem),
        scratch_shapes=[
            pltpu.VMEM((rows, width), BF16), pltpu.VMEM((rows, width), BF16),
            pltpu.VMEM(small, F32), pltpu.VMEM(small, F32), pltpu.VMEM((rows, width), F32),
            dma((2,)), dma((chunks,)), dma, dma((chunks,)),
            states, states, states, states, states, states,
            pltpu.VMEM((groups * modes, rows), F32),
            pltpu.VMEM((width // tile, rows, tile // (width // groups) * modes), BF16),
            pltpu.VMEM((width // tile, rows, tile // (width // groups) * modes), BF16),
            pltpu.VMEM((modes, width), F32),
            pltpu.VMEM(small, F32),
            pltpu.VMEM(small, F32),
            pltpu.VMEM((seqs - 1,) + small, F32),
            pltpu.VMEM(small, F32),
            pltpu.VMEM((shards - 1,) + small, F32),
            dma((chunks,)), dma((chunks,)), dma((chunks,)), dma((chunks,)),
            dma((seqs - 1,)), dma((seqs - 1,)), dma((shards - 1,)), dma((shards - 1,)),
        ],
        compiler_params=pltpu.CompilerParams(
            collective_id=0, has_side_effects=True, vmem_limit_bytes=63 * 1024 * 1024
        ),
    )(grad_out[0], inputs[0], residues, rates)
    span = width // 8
    piece = pl.BlockSpec((rows, span), lambda i: (0, i))
    whole = pl.BlockSpec(small, lambda i: (0, 0))
    grad_in, total = pl.pallas_call(
        functools.partial(write, float(seqs * shards * rows * (width // groups))),
        grid=(width // span,),
        out_shape=(jax.ShapeDtypeStruct((rows, width), F32), jax.ShapeDtypeStruct(small, F32)),
        in_specs=[piece, whole, whole],
        out_specs=(piece, whole),
        compiler_params=pltpu.CompilerParams(vmem_limit_bytes=63 * 1024 * 1024),
    )(grad_in, total, rates)
    return grad_in[None], total


def solution(mesh):
    placed = (P("seq", "ctx", None), P("seq", "ctx", None), P(), P())
    return jax.shard_map(
        functools.partial(local, mesh.shape["ctx"], mesh.shape["seq"]),
        mesh=mesh, in_specs=placed, out_specs=(P("seq", "ctx", None), P()), check_vma=False,
    )
```

```python
import functools

import jax
import jax.numpy as jnp
from jax import lax
from jax.experimental import pallas as pl
from jax.experimental.pallas import tpu as pltpu
from jax.sharding import PartitionSpec as P

MESH = pl.DeviceIdType.MESH
F32 = jnp.float32
BF16 = jnp.bfloat16


def dot(a, b):
    return jnp.dot(a, b, preferred_element_type=F32)


def split(a):
    high = a.astype(BF16)
    return high, (a - high.astype(F32)).astype(BF16)


def one_minus_exp(u):
    series = 1.0 - u * (1.0 / 8.0)
    for order in (7.0, 6.0, 5.0, 4.0, 3.0, 2.0):
        series = 1.0 - u * (1.0 / order) * series
    return u * series


def body(
    shards, seqs, chunks, grad_hbm, in_hbm, res_hbm, rate_hbm, out_hbm, total_ref,
    grad_ref, in_ref, res_ref, rate_ref, out_ref, small_sem, grad_sem, in_sem, out_sem,
    own, pair, joined, incoming, outgoing, decay_pow, decay, tail_high, tail_low, tail, lag_sums,
    partial, from_seq, seq_sum, from_ctx,
    pair_send, pair_recv, chain_send, chain_recv, seq_send, seq_recv, ctx_send, ctx_recv,
):
    rows, width = grad_ref.shape
    modes, groups = res_ref.shape
    per_group = width // groups
    tile_groups = modes if modes * per_group == 256 else 256 // per_group
    tile = tile_groups * per_group
    tiles = width // tile
    chunk_tiles = tiles // chunks
    half = 128
    half_groups = half // per_group
    stacked = tile_groups * modes
    pairs = shards // 2

    span = width // chunks
    rate_copy = pltpu.make_async_copy(rate_hbm, rate_ref, small_sem.at[0])
    res_copy = pltpu.make_async_copy(res_hbm, res_ref, small_sem.at[1])
    in_copy = pltpu.make_async_copy(in_hbm, in_ref, in_sem)
    grad_copies = [
        pltpu.make_async_copy(
            grad_hbm.at[:, q * span : (q + 1) * span],
            grad_ref.at[:, q * span : (q + 1) * span],
            grad_sem.at[q],
        )
        for q in range(chunks)
    ]
    rate_copy.start()
    for copy in grad_copies:
        copy.start()
    in_copy.start()
    res_copy.start()

    me = lax.axis_index("ctx")
    my_seq = lax.axis_index("seq")
    upper = me % 2
    place = me // 2
    partner = me + 1 - 2 * upper
    hops = pairs - 1 - place

    barrier = pltpu.get_barrier_semaphore()
    for offset in range(1, shards):
        pl.semaphore_signal(
            barrier, inc=1, device_id={"ctx": lax.rem(me + offset, shards)}, device_id_type=MESH
        )
    for offset in range(1, seqs):
        pl.semaphore_signal(
            barrier, inc=1, device_id={"seq": lax.rem(my_seq + offset, seqs)}, device_id_type=MESH
        )

    lane_group = lax.broadcasted_iota(jnp.int32, (modes, tile), 1) // per_group
    ahead = lax.broadcasted_iota(jnp.int32, (modes, rows), 1).astype(F32)
    behind = float(rows) - ahead

    def rolled(values, index):
        return pltpu.roll(values, lax.rem(groups - index * tile_groups, groups), 1)

    def compress(wide):
        kept = jnp.zeros((modes, tile), F32)
        for g in range(tile_groups):
            kept = jnp.where(lane_group == g, wide[g * modes : (g + 1) * modes, :], kept)
        return kept

    def lanes(index, size):
        if isinstance(index, int):
            return pl.ds(index * size, size)
        return pl.ds(pl.multiple_of(index * size, size), size)

    def pair_copy(q):
        return pltpu.make_async_remote_copy(
            own.at[q], pair.at[q], pair_send.at[q], pair_recv.at[q],
            device_id={"ctx": partner}, device_id_type=MESH,
        )

    def chain_copy(q):
        return pltpu.make_async_remote_copy(
            outgoing.at[q], incoming.at[q], chain_send.at[q], chain_recv.at[q],
            device_id={"ctx": lax.rem(me + shards - 2, shards)}, device_id_type=MESH,
        )

    rate_copy.wait()
    for q in range(chunks):
        grad_copies[q].wait()

        def summarize(step, carry, q=q):
            index = q * chunk_tiles + step
            rates = rolled(rate_ref[...], index)
            spread = jnp.zeros((modes, tile), F32)
            parts = []
            for g in range(tile_groups):
                rate = rates[:, g : g + 1]
                parts.append(jnp.exp(-rate * ahead))
                spread = jnp.where(lane_group == g, rate, spread)
            decays = jnp.concatenate(parts, axis=0)
            decay[lanes(index, stacked), :] = decays
            high, low = split(decays)
            grads = grad_ref[:, lanes(index, tile)]
            wide = dot(jnp.concatenate([high, low], axis=1), jnp.concatenate([grads, grads], axis=0))
            own[q, :, lanes(step, tile)] = compress(wide)
            decay_pow[q, :, lanes(step, tile)] = jnp.exp(-float(rows) * spread)
            return carry

        lax.fori_loop(0, chunk_tiles, summarize, 0, unroll=True)
        if q == 0:
            pl.semaphore_wait(barrier, shards - 1 + seqs - 1)
        pair_copy(q).start()

    in_copy.wait()
    res_copy.wait()

    def exchange(step):
        @pl.when(step < chunks)
        def _():
            pair_copy(step).wait_recv()
            power = decay_pow[step]
            mine, other = own[step], pair[step]
            near = jnp.where(upper == 0, mine, other)
            far = jnp.where(upper == 0, other, mine)
            joined[step] = near + power * far

            @pl.when(hops == 0)
            def _():
                incoming[step] = jnp.zeros(incoming.shape[1:], F32)
                if pairs > 1:
                    outgoing[step] = joined[step]
                    chain_copy(step).start()

        if pairs > 1:
            q = step - hops

            @pl.when((hops > 0) & (q >= 0) & (q < chunks))
            def _():
                chain_copy(q).wait_recv()

                @pl.when(place > 0)
                def _():
                    power = decay_pow[q]
                    outgoing[q] = joined[q] + power * power * incoming[q]
                    chain_copy(q).start()

    steps = chunks + pairs - 1

    sub = min(32, rows)
    subs = rows // sub
    sub_lane_group = lax.broadcasted_iota(jnp.int32, (sub, half), 1) // per_group
    folded_masks = []
    for g in range(half_groups):
        mask = jnp.where(sub_lane_group == g, 1.0, 0.0).astype(BF16)
        folded_masks.append(jnp.concatenate([mask] * subs, axis=1))
    tile_masks = [jnp.where(lane_group == g, 1.0, 0.0).astype(BF16) for g in range(tile_groups)]
    row_of = lax.broadcasted_iota(jnp.int32, (rows, rows), 0)
    col_of = lax.broadcasted_iota(jnp.int32, (rows, rows), 1)
    sub_row = lax.broadcasted_iota(jnp.int32, (sub, rows), 0)
    sub_col = lax.broadcasted_iota(jnp.int32, (sub, rows), 1)
    causal = sub_col >= sub_row
    inside = sub_col <= rows - sub + sub_row
    mirrored = (row_of // sub == col_of // sub) & (
        lax.rem(row_of, sub) + lax.rem(col_of, sub) == sub - 1
    )
    reverse = jnp.where(mirrored, 1.0, 0.0).astype(BF16)
    group_lane = lax.broadcasted_iota(jnp.int32, (modes, groups), 1)
    amplitude = res_ref[...] * jnp.sqrt(one_minus_exp(2.0 * rate_ref[...]) * (1.0 / modes))
    lag_sums[...] = jnp.zeros_like(lag_sums)

    def folded_rows(grads):
        return jnp.concatenate(
            [grads]
            + [
                jnp.concatenate([grads[r * sub :], jnp.zeros((r * sub, half), BF16)], axis=0)
                for r in range(1, subs)
            ],
            axis=1,
        )

    def group_decays(index, g):
        start = index * stacked + g * modes
        return decay[pl.ds(start if isinstance(start, int) else pl.multiple_of(start, modes), modes), :]

    def correlate(index):
        rates = rolled(rate_ref[...], index)
        amps = rolled(amplitude, index)
        tails = []
        weights = []
        sums = lag_sums[...]
        for part in range(tile // half):
            where_half = lanes(index * (tile // half) + part, half)
            shifted = folded_rows(grad_ref[:, where_half])
            ins = dot(reverse, in_ref[:, where_half]).astype(BF16)
            folded = jnp.concatenate([ins[r * sub : (r + 1) * sub] for r in range(subs)], axis=1)
            products = lax.dot_general(
                jnp.concatenate([folded * mask for mask in folded_masks], axis=0),
                shifted, (((1,), (1,)), ((), ())), preferred_element_type=F32,
            )
            for g8 in range(half_groups):
                g = part * half_groups + g8
                skewed = pltpu.roll(
                    products[g8 * sub : (g8 + 1) * sub], rows + 1 - sub, 1, stride=1, stride_axis=0
                )
                lagged = jnp.sum(jnp.where(inside, skewed, 0.0), axis=0, keepdims=True)
                value = jnp.sum(group_decays(index, g) * lagged, axis=1, keepdims=True)
                sums = jnp.where(group_lane == index * tile_groups + g, value, sums)
                remaining = jnp.exp(-rates[:, g : g + 1] * behind)
                tails.append(remaining)
                weights.append(amps[:, g : g + 1] * remaining)
        lag_sums[...] = sums
        high, low = split(jnp.concatenate(tails, axis=0))
        ins = in_ref[:, lanes(index, tile)]
        wide = dot(jnp.concatenate([high, low], axis=1), jnp.concatenate([ins, ins], axis=0))
        tail[:, lanes(index, tile)] = compress(wide)
        high, low = split(jnp.concatenate(weights, axis=0).T)
        tail_high[index] = high
        tail_low[index] = low

    def carried(index):
        q, inner = index // chunk_tiles, lax.rem(index, chunk_tiles)
        high, low = split(incoming[q, :, lanes(inner, tile)])
        left = tail_high[index]
        both = dot(
            jnp.concatenate([left, tail_low[index]], axis=0),
            jnp.concatenate([high * mask for mask in tile_masks], axis=0),
        )
        rest = dot(left, jnp.concatenate([low * mask for mask in tile_masks], axis=0))
        return both[:rows] + both[rows:] + rest

    def convolve(index, entered=None):
        amps = rolled(amplitude, index)
        for part in range(tile // half):
            where_half = lanes(index * (tile // half) + part, half)
            shifted = folded_rows(grad_ref[:, where_half])
            filters = []
            for g8 in range(half_groups):
                g = part * half_groups + g8
                filt = jnp.sum(amps[:, g : g + 1] * group_decays(index, g), axis=0, keepdims=True)
                toeplitz = pltpu.roll(
                    jnp.broadcast_to(filt, (sub, rows)), 0, 1, stride=1, stride_axis=0
                )
                high, low = split(jnp.where(causal, toeplitz, 0.0))
                filters.append(jnp.concatenate([high, low], axis=1))
            wide = dot(jnp.concatenate(filters, axis=0), jnp.concatenate([shifted, shifted], axis=0))
            for r in range(subs):
                result = wide[:sub, r * half : (r + 1) * half]
                for g8 in range(1, half_groups):
                    piece = wide[g8 * sub : (g8 + 1) * sub, r * half : (r + 1) * half]
                    result = jnp.where(sub_lane_group == g8, piece, result)
                if entered is not None:
                    result += entered[r * sub : (r + 1) * sub, part * half : (part + 1) * half]
                out_ref[r * sub : (r + 1) * sub, where_half] = result

    assert tiles % 4 == 0 and chunks % 2 == 0

    def first(step, carry):
        for inner in range(2):
            correlate(step * 2 + inner)
        exchange(step)
        return carry

    def second(step, carry):
        for inner in range(2):
            convolve(step * 2 + inner)
        exchange(tiles // 2 + step)
        return carry

    lax.fori_loop(0, tiles // 2, first, 0)
    lax.fori_loop(0, tiles // 4, second, 0)
    for step in range(tiles // 2 + tiles // 4, steps):
        exchange(step)

    def enter(index, sums):
        q, inner = index // chunk_tiles, lax.rem(index, chunk_tiles)
        entry = incoming[q, :, lanes(inner, tile)]
        power = decay_pow[q, :, lanes(inner, tile)]
        entry = jnp.where(upper == 0, pair[q, :, lanes(inner, tile)] + power * entry, entry)
        incoming[q, :, lanes(inner, tile)] = entry
        value = tail[:, lanes(index, tile)] * entry
        high = value.astype(BF16)
        rest = value - high.astype(F32)
        middle, low = split(rest)
        chan_group = lax.broadcasted_iota(jnp.int32, (tile, groups), 0) // per_group
        member = lax.broadcasted_iota(jnp.int32, (tile, groups), 1) == chan_group + index * tile_groups
        member = jnp.where(member, 1.0, 0.0).astype(BF16)
        found = dot(jnp.concatenate([high, middle, low], axis=0), member)
        return sums + found[:modes] + found[modes : 2 * modes] + found[2 * modes :]

    partial[...] = lax.fori_loop(0, tiles, enter, lag_sums[...], unroll=4)

    def seq_copy(offset):
        return pltpu.make_async_remote_copy(
            partial, from_seq.at[offset - 1], seq_send.at[offset - 1], seq_recv.at[offset - 1],
            device_id={"seq": lax.rem(my_seq + offset, seqs)}, device_id_type=MESH,
        )

    def ctx_copy(offset):
        return pltpu.make_async_remote_copy(
            seq_sum, from_ctx.at[offset - 1], ctx_send.at[offset - 1], ctx_recv.at[offset - 1],
            device_id={"ctx": lax.rem(me + offset, shards)}, device_id_type=MESH,
        )

    for offset in range(1, seqs):
        seq_copy(offset).start()

    def out_copy(q):
        return pltpu.make_async_copy(
            out_ref.at[:, q * span : (q + 1) * span],
            out_hbm.at[:, q * span : (q + 1) * span],
            out_sem.at[q],
        )

    def finish(q):
        for index in range(q * chunk_tiles, (q + 1) * chunk_tiles):
            if index < tiles // 2:
                out_ref[:, lanes(index, tile)] += carried(index)
            else:
                convolve(index, carried(index))
        out_copy(q).start()

    for q in range(chunks // 2, 3 * chunks // 4):
        finish(q)
    for offset in range(1, seqs):
        seq_copy(offset).wait_recv()

    def ordered(mine, received, place_here, count):
        added = jnp.zeros((modes, groups), F32)
        for source in range(count):
            value = jnp.where(place_here == source, mine, 0.0)
            for offset in range(1, count):
                value = jnp.where(
                    lax.rem(source + offset, count) == place_here, received[offset - 1], value
                )
            added = added + value
        return added

    seq_sum[...] = ordered(partial[...], from_seq, my_seq, seqs)
    for offset in range(1, shards):
        ctx_copy(offset).start()
    for q in range(3 * chunks // 4, chunks):
        finish(q)
    for q in range(chunks // 2):
        finish(q)
    for offset in range(1, shards):
        ctx_copy(offset).wait_recv()

    def gather_sum(source, added):
        offset = lax.rem(me - source + shards, shards)
        slot = jnp.maximum(offset - 1, 0)
        return added + jnp.where(offset == 0, seq_sum[...], from_ctx[slot])

    total = lax.fori_loop(0, shards, gather_sum, jnp.zeros((modes, groups), F32))
    scale = 1.0 / float(seqs * shards * rows * per_group)
    total_ref[...] = total * jnp.sqrt(one_minus_exp(2.0 * rate_ref[...]) * scale)

    for q in range(chunks):
        out_copy(q).wait()
        pair_copy(q).wait_send()
        if pairs > 1:
            @pl.when(place > 0)
            def _(q=q):
                chain_copy(q).wait_send()
    for offset in range(1, seqs):
        seq_copy(offset).wait_send()
    for offset in range(1, shards):
        ctx_copy(offset).wait_send()


def local(shards, seqs, grad_out, inputs, residues, rates):
    rows, width = grad_out.shape[1:]
    modes, groups = residues.shape
    chunks = 8
    tile = 256
    chunk_shape = (chunks, modes, width // chunks)
    small = (modes, groups)
    states = pltpu.VMEM(chunk_shape, F32)
    dma = pltpu.SemaphoreType.DMA
    vmem = pl.BlockSpec(memory_space=pltpu.VMEM)
    grad_in, total = pl.pallas_call(
        functools.partial(body, shards, seqs, chunks),
        out_shape=(
            jax.ShapeDtypeStruct((rows, width), F32),
            jax.ShapeDtypeStruct(small, F32),
        ),
        in_specs=[pl.BlockSpec(memory_space=pltpu.HBM)] * 4,
        out_specs=(pl.BlockSpec(memory_space=pltpu.HBM), vmem),
        scratch_shapes=[
            pltpu.VMEM((rows, width), BF16), pltpu.VMEM((rows, width), BF16),
            pltpu.VMEM(small, F32), pltpu.VMEM(small, F32), pltpu.VMEM((rows, width), F32),
            dma((2,)), dma((chunks,)), dma, dma((chunks,)),
            states, states, states, states, states, states,
            pltpu.VMEM((groups * modes, rows), F32),
            pltpu.VMEM((width // tile, rows, tile // (width // groups) * modes), BF16),
            pltpu.VMEM((width // tile, rows, tile // (width // groups) * modes), BF16),
            pltpu.VMEM((modes, width), F32),
            pltpu.VMEM(small, F32),
            pltpu.VMEM(small, F32),
            pltpu.VMEM((seqs - 1,) + small, F32),
            pltpu.VMEM(small, F32),
            pltpu.VMEM((shards - 1,) + small, F32),
            dma((chunks,)), dma((chunks,)), dma((chunks,)), dma((chunks,)),
            dma((seqs - 1,)), dma((seqs - 1,)), dma((shards - 1,)), dma((shards - 1,)),
        ],
        compiler_params=pltpu.CompilerParams(
            collective_id=0, has_side_effects=True, vmem_limit_bytes=63 * 1024 * 1024
        ),
    )(grad_out[0], inputs[0], residues, rates)
    return grad_in[None], total


def solution(mesh):
    placed = (P("seq", "ctx", None), P("seq", "ctx", None), P(), P())
    return jax.shard_map(
        functools.partial(local, mesh.shape["ctx"], mesh.shape["seq"]),
        mesh=mesh, in_specs=placed, out_specs=(P("seq", "ctx", None), P()), check_vma=False,
    )
```

```python
import functools

import jax
import jax.numpy as jnp
from jax import lax
from jax.experimental import pallas as pl
from jax.experimental.pallas import tpu as pltpu
from jax.sharding import PartitionSpec as P

MESH = pl.DeviceIdType.MESH
F32 = jnp.float32
BF16 = jnp.bfloat16


def dot(a, b):
    return jnp.dot(a, b, preferred_element_type=F32)


def split(a):
    high = a.astype(BF16)
    return high, (a - high.astype(F32)).astype(BF16)


def one_minus_exp(u):
    series = 1.0 - u * (1.0 / 8.0)
    for order in (7.0, 6.0, 5.0, 4.0, 3.0, 2.0):
        series = 1.0 - u * (1.0 / order) * series
    return u * series


def body(
    shards, seqs, chunks, grad_hbm, in_hbm, res_hbm, rate_hbm, out_hbm, total_ref,
    grad_ref, in_ref, res_ref, rate_ref, out_ref, small_sem, grad_sem, in_sem, out_sem,
    own, pair, joined, incoming, outgoing, decay_pow, decay, tail_high, tail_low, tail, lag_sums,
    partial, from_seq, seq_sum, from_ctx,
    pair_send, pair_recv, chain_send, chain_recv, seq_send, seq_recv, ctx_send, ctx_recv,
):
    rows, width = grad_ref.shape
    modes, groups = res_ref.shape
    per_group = width // groups
    tile_groups = modes if modes * per_group == 256 else 256 // per_group
    tile = tile_groups * per_group
    tiles = width // tile
    chunk_tiles = tiles // chunks
    half = 128
    half_groups = half // per_group
    stacked = tile_groups * modes
    pairs = shards // 2

    span = width // chunks
    rate_copy = pltpu.make_async_copy(rate_hbm, rate_ref, small_sem.at[0])
    res_copy = pltpu.make_async_copy(res_hbm, res_ref, small_sem.at[1])
    in_copy = pltpu.make_async_copy(in_hbm, in_ref, in_sem)
    def grad_copy(q):
        where = pl.ds(pl.multiple_of(q * span, span), span)
        return pltpu.make_async_copy(grad_hbm.at[:, where], grad_ref.at[:, where], grad_sem.at[q])

    rate_copy.start()
    for q in range(chunks):
        grad_copy(q).start()
    in_copy.start()
    res_copy.start()

    me = lax.axis_index("ctx")
    my_seq = lax.axis_index("seq")
    upper = me % 2
    place = me // 2
    partner = me + 1 - 2 * upper
    hops = pairs - 1 - place

    barrier = pltpu.get_barrier_semaphore()
    for offset in range(1, shards):
        pl.semaphore_signal(
            barrier, inc=1, device_id={"ctx": lax.rem(me + offset, shards)}, device_id_type=MESH
        )
    for offset in range(1, seqs):
        pl.semaphore_signal(
            barrier, inc=1, device_id={"seq": lax.rem(my_seq + offset, seqs)}, device_id_type=MESH
        )

    lane_group = lax.broadcasted_iota(jnp.int32, (modes, tile), 1) // per_group
    ahead = lax.broadcasted_iota(jnp.int32, (modes, rows), 1).astype(F32)
    behind = float(rows) - ahead

    def rolled(values, index):
        return pltpu.roll(values, lax.rem(groups - index * tile_groups, groups), 1)

    def compress(wide):
        kept = jnp.zeros((modes, tile), F32)
        for g in range(tile_groups):
            kept = jnp.where(lane_group == g, wide[g * modes : (g + 1) * modes, :], kept)
        return kept

    def lanes(index, size):
        return pl.ds(pl.multiple_of(index * size, size), size)

    def pair_copy(q):
        return pltpu.make_async_remote_copy(
            own.at[q], pair.at[q], pair_send.at[q], pair_recv.at[q],
            device_id={"ctx": partner}, device_id_type=MESH,
        )

    def chain_copy(q):
        return pltpu.make_async_remote_copy(
            outgoing.at[q], incoming.at[q], chain_send.at[q], chain_recv.at[q],
            device_id={"ctx": lax.rem(me + shards - 2, shards)}, device_id_type=MESH,
        )

    rate_copy.wait()
    def summaries(q, carry):
        grad_copy(q).wait()

        def summarize(step, carry):
            index = q * chunk_tiles + step
            rates = rolled(rate_ref[...], index)
            spread = jnp.zeros((modes, tile), F32)
            parts = []
            for g in range(tile_groups):
                rate = rates[:, g : g + 1]
                parts.append(jnp.exp(-rate * ahead))
                spread = jnp.where(lane_group == g, rate, spread)
            decays = jnp.concatenate(parts, axis=0)
            decay[lanes(index, stacked), :] = decays
            high, low = split(decays)
            grads = grad_ref[:, lanes(index, tile)]
            wide = dot(jnp.concatenate([high, low], axis=1), jnp.concatenate([grads, grads], axis=0))
            own[q, :, lanes(step, tile)] = compress(wide)
            decay_pow[q, :, lanes(step, tile)] = jnp.exp(-float(rows) * spread)
            return carry

        lax.fori_loop(0, chunk_tiles, summarize, 0, unroll=True)

        @pl.when(q == 0)
        def _():
            pl.semaphore_wait(barrier, shards - 1 + seqs - 1)

        pair_copy(q).start()
        return carry

    lax.fori_loop(0, chunks, summaries, 0)

    in_copy.wait()
    res_copy.wait()

    def exchange(step):
        @pl.when(step < chunks)
        def _():
            pair_copy(step).wait_recv()
            power = decay_pow[step]
            mine, other = own[step], pair[step]
            near = jnp.where(upper == 0, mine, other)
            far = jnp.where(upper == 0, other, mine)
            joined[step] = near + power * far

            @pl.when(hops == 0)
            def _():
                incoming[step] = jnp.zeros(incoming.shape[1:], F32)
                if pairs > 1:
                    outgoing[step] = joined[step]
                    chain_copy(step).start()

        if pairs > 1:
            q = step - hops

            @pl.when((hops > 0) & (q >= 0) & (q < chunks))
            def _():
                chain_copy(q).wait_recv()

                @pl.when(place > 0)
                def _():
                    power = decay_pow[q]
                    outgoing[q] = joined[q] + power * power * incoming[q]
                    chain_copy(q).start()

    steps = chunks + pairs - 1
    per_step = max(1, tiles // steps)

    sub = min(32, rows)
    subs = rows // sub
    sub_lane_group = lax.broadcasted_iota(jnp.int32, (sub, half), 1) // per_group
    folded_group = lax.rem(
        lax.broadcasted_iota(jnp.int32, (sub, subs * half), 1), half
    ) // per_group
    row_of = lax.broadcasted_iota(jnp.int32, (rows, rows), 0)
    col_of = lax.broadcasted_iota(jnp.int32, (rows, rows), 1)
    sub_row = lax.broadcasted_iota(jnp.int32, (sub, rows), 0)
    sub_col = lax.broadcasted_iota(jnp.int32, (sub, rows), 1)
    causal = sub_col >= sub_row
    inside = sub_col <= rows - sub + sub_row
    mirrored = (row_of // sub == col_of // sub) & (
        lax.rem(row_of, sub) + lax.rem(col_of, sub) == sub - 1
    )
    reverse = jnp.where(mirrored, 1.0, 0.0).astype(BF16)
    group_lane = lax.broadcasted_iota(jnp.int32, (modes, groups), 1)
    amplitude = res_ref[...] * jnp.sqrt(one_minus_exp(2.0 * rate_ref[...]) * (1.0 / modes))
    lag_sums[...] = jnp.zeros_like(lag_sums)

    def convolve(index, carry):
        rates = rolled(rate_ref[...], index)
        amps = rolled(amplitude, index)
        tails = []
        weights = []
        sums = lag_sums[...]
        for part in range(tile // half):
            where_half = lanes(index * (tile // half) + part, half)
            grads = grad_ref[:, where_half]
            ins = dot(reverse, in_ref[:, where_half]).astype(BF16)
            shifted = jnp.concatenate(
                [grads]
                + [
                    jnp.concatenate(
                        [grads[r * sub :], jnp.zeros((r * sub, half), BF16)], axis=0
                    )
                    for r in range(1, subs)
                ],
                axis=1,
            )
            folded = jnp.concatenate([ins[r * sub : (r + 1) * sub] for r in range(subs)], axis=1)
            filters, masked, kept = [], [], []
            for g8 in range(half_groups):
                g = part * half_groups + g8
                rate = rates[:, g : g + 1]
                amp = amps[:, g : g + 1]
                decays = decay[pl.ds(pl.multiple_of(index * stacked + g * modes, modes), modes), :]
                kept.append(decays)
                filt = jnp.sum(amp * decays, axis=0, keepdims=True)
                toeplitz = pltpu.roll(
                    jnp.broadcast_to(filt, (sub, rows)), 0, 1, stride=1, stride_axis=0
                )
                high, low = split(jnp.where(causal, toeplitz, 0.0))
                filters.append(jnp.concatenate([high, low], axis=1))
                masked.append(jnp.where(folded_group == g8, folded, jnp.zeros_like(folded)))
                remaining = jnp.exp(-rate * behind)
                tails.append(remaining)
                weights.append(amp * remaining)
            wide = dot(jnp.concatenate(filters, axis=0), jnp.concatenate([shifted, shifted], axis=0))
            for r in range(subs):
                result = jnp.zeros((sub, half), F32)
                for g8 in range(half_groups):
                    piece = wide[g8 * sub : (g8 + 1) * sub, r * half : (r + 1) * half]
                    result = jnp.where(sub_lane_group == g8, piece, result)
                out_ref[r * sub : (r + 1) * sub, where_half] = result
            products = lax.dot_general(
                jnp.concatenate(masked, axis=0), shifted, (((1,), (1,)), ((), ())),
                preferred_element_type=F32,
            )
            for g8 in range(half_groups):
                g = part * half_groups + g8
                skewed = pltpu.roll(
                    products[g8 * sub : (g8 + 1) * sub], rows + 1 - sub, 1, stride=1, stride_axis=0
                )
                lagged = jnp.sum(jnp.where(inside, skewed, 0.0), axis=0, keepdims=True)
                value = jnp.sum(kept[g8] * lagged, axis=1, keepdims=True)
                sums = jnp.where(group_lane == index * tile_groups + g, value, sums)
        lag_sums[...] = sums
        high, low = split(jnp.concatenate(tails, axis=0))
        ins = in_ref[:, lanes(index, tile)]
        wide = dot(jnp.concatenate([high, low], axis=1), jnp.concatenate([ins, ins], axis=0))
        tail[:, lanes(index, tile)] = compress(wide)
        high, low = split(jnp.concatenate(weights, axis=0).T)
        tail_high[index] = high
        tail_low[index] = low

        return carry

    def advance(step, carry):
        for inner in range(per_step):
            convolve(step * per_step + inner, 0)
        exchange(step)
        return carry

    lax.fori_loop(0, tiles // per_step, advance, 0)
    for index in range(tiles // per_step * per_step, tiles):
        convolve(index, 0)
    for step in range(tiles // per_step, steps):
        exchange(step)

    def enter(index, sums):
        q, inner = index // chunk_tiles, lax.rem(index, chunk_tiles)
        entry = incoming[q, :, lanes(inner, tile)]
        power = decay_pow[q, :, lanes(inner, tile)]
        entry = jnp.where(upper == 0, pair[q, :, lanes(inner, tile)] + power * entry, entry)
        incoming[q, :, lanes(inner, tile)] = entry
        value = tail[:, lanes(index, tile)] * entry
        high = value.astype(BF16)
        rest = value - high.astype(F32)
        middle, low = split(rest)
        chan_group = lax.broadcasted_iota(jnp.int32, (tile, groups), 0) // per_group
        member = lax.broadcasted_iota(jnp.int32, (tile, groups), 1) == chan_group + index * tile_groups
        member = jnp.where(member, 1.0, 0.0).astype(BF16)
        found = dot(jnp.concatenate([high, middle, low], axis=0), member)
        return sums + found[:modes] + found[modes : 2 * modes] + found[2 * modes :]

    partial[...] = lax.fori_loop(0, tiles, enter, lag_sums[...], unroll=4)

    def seq_copy(offset):
        return pltpu.make_async_remote_copy(
            partial, from_seq.at[offset - 1], seq_send.at[offset - 1], seq_recv.at[offset - 1],
            device_id={"seq": lax.rem(my_seq + offset, seqs)}, device_id_type=MESH,
        )

    def ctx_copy(offset):
        return pltpu.make_async_remote_copy(
            seq_sum, from_ctx.at[offset - 1], ctx_send.at[offset - 1], ctx_recv.at[offset - 1],
            device_id={"ctx": lax.rem(me + offset, shards)}, device_id_type=MESH,
        )

    for offset in range(1, seqs):
        seq_copy(offset).start()

    def carry_in(index, carry):
        q, inner = index // chunk_tiles, lax.rem(index, chunk_tiles)
        entry = incoming[q, :, lanes(inner, tile)]
        high, low = split(entry)

        def blocks(value):
            return jnp.concatenate(
                [jnp.where(lane_group == g, value, jnp.zeros_like(value)) for g in range(tile_groups)],
                axis=0,
            )

        left = tail_high[index]
        both = dot(jnp.concatenate([left, tail_low[index]], axis=0), blocks(high))
        rest = dot(left, blocks(low))
        out_ref[:, lanes(index, tile)] += both[:rows] + both[rows:] + rest
        return carry

    def out_copy(q):
        return pltpu.make_async_copy(
            out_ref.at[:, pl.ds(pl.multiple_of(q * span, span), span)],
            out_hbm.at[:, pl.ds(pl.multiple_of(q * span, span), span)],
            out_sem.at[q],
        )

    def finish(q, carry):
        lax.fori_loop(
            0, chunk_tiles, lambda step, c: carry_in(q * chunk_tiles + step, c), 0, unroll=True
        )
        out_copy(q).start()
        return carry

    lax.fori_loop(0, chunks // 2, finish, 0)
    for offset in range(1, seqs):
        seq_copy(offset).wait_recv()

    def ordered(mine, received, place_here, count):
        added = jnp.zeros((modes, groups), F32)
        for source in range(count):
            value = jnp.where(place_here == source, mine, 0.0)
            for offset in range(1, count):
                value = jnp.where(
                    lax.rem(source + offset, count) == place_here, received[offset - 1], value
                )
            added = added + value
        return added

    seq_sum[...] = ordered(partial[...], from_seq, my_seq, seqs)
    for offset in range(1, shards):
        ctx_copy(offset).start()
    lax.fori_loop(chunks // 2, chunks, finish, 0)
    for offset in range(1, shards):
        ctx_copy(offset).wait_recv()

    def gather_sum(source, added):
        offset = lax.rem(me - source + shards, shards)
        slot = jnp.maximum(offset - 1, 0)
        return added + jnp.where(offset == 0, seq_sum[...], from_ctx[slot])

    total = lax.fori_loop(0, shards, gather_sum, jnp.zeros((modes, groups), F32))
    scale = 1.0 / float(seqs * shards * rows * per_group)
    total_ref[...] = total * jnp.sqrt(one_minus_exp(2.0 * rate_ref[...]) * scale)

    for q in range(chunks):
        out_copy(q).wait()
        pair_copy(q).wait_send()
        if pairs > 1:
            @pl.when(place > 0)
            def _(q=q):
                chain_copy(q).wait_send()
    for offset in range(1, seqs):
        seq_copy(offset).wait_send()
    for offset in range(1, shards):
        ctx_copy(offset).wait_send()


def local(shards, seqs, grad_out, inputs, residues, rates):
    rows, width = grad_out.shape[1:]
    modes, groups = residues.shape
    chunks = 4
    tile = 256
    chunk_shape = (chunks, modes, width // chunks)
    small = (modes, groups)
    states = pltpu.VMEM(chunk_shape, F32)
    dma = pltpu.SemaphoreType.DMA
    vmem = pl.BlockSpec(memory_space=pltpu.VMEM)
    grad_in, total = pl.pallas_call(
        functools.partial(body, shards, seqs, chunks),
        out_shape=(
            jax.ShapeDtypeStruct((rows, width), F32),
            jax.ShapeDtypeStruct(small, F32),
        ),
        in_specs=[pl.BlockSpec(memory_space=pltpu.HBM)] * 4,
        out_specs=(pl.BlockSpec(memory_space=pltpu.HBM), vmem),
        scratch_shapes=[
            pltpu.VMEM((rows, width), BF16), pltpu.VMEM((rows, width), BF16),
            pltpu.VMEM(small, F32), pltpu.VMEM(small, F32), pltpu.VMEM((rows, width), F32),
            dma((2,)), dma((chunks,)), dma, dma((chunks,)),
            states, states, states, states, states, states,
            pltpu.VMEM((groups * modes, rows), F32),
            pltpu.VMEM((width // tile, rows, tile // (width // groups) * modes), BF16),
            pltpu.VMEM((width // tile, rows, tile // (width // groups) * modes), BF16),
            pltpu.VMEM((modes, width), F32),
            pltpu.VMEM(small, F32),
            pltpu.VMEM(small, F32),
            pltpu.VMEM((seqs - 1,) + small, F32),
            pltpu.VMEM(small, F32),
            pltpu.VMEM((shards - 1,) + small, F32),
            dma((chunks,)), dma((chunks,)), dma((chunks,)), dma((chunks,)),
            dma((seqs - 1,)), dma((seqs - 1,)), dma((shards - 1,)), dma((shards - 1,)),
        ],
        compiler_params=pltpu.CompilerParams(
            collective_id=0, has_side_effects=True, vmem_limit_bytes=63 * 1024 * 1024
        ),
    )(grad_out[0], inputs[0], residues, rates)
    return grad_in[None], total


def solution(mesh):
    placed = (P("seq", "ctx", None), P("seq", "ctx", None), P(), P())
    return jax.shard_map(
        functools.partial(local, mesh.shape["ctx"], mesh.shape["seq"]),
        mesh=mesh, in_specs=placed, out_specs=(P("seq", "ctx", None), P()), check_vma=False,
    )
```

```python
import functools

import jax
import jax.numpy as jnp
from jax import lax
from jax.experimental import pallas as pl
from jax.experimental.pallas import tpu as pltpu
from jax.sharding import PartitionSpec as P

MESH = pl.DeviceIdType.MESH
F32 = jnp.float32
BF16 = jnp.bfloat16


def dot(a, b):
    return jnp.dot(a, b, preferred_element_type=F32)


def split(a):
    high = a.astype(BF16)
    return high, (a - high.astype(F32)).astype(BF16)


def one_minus_exp(u):
    series = 1.0 - u * (1.0 / 8.0)
    for order in (7.0, 6.0, 5.0, 4.0, 3.0, 2.0):
        series = 1.0 - u * (1.0 / order) * series
    return u * series


def body(
    shards, seqs, chunks, grad_hbm, in_hbm, res_hbm, rate_hbm, out_hbm, total_ref,
    grad_ref, in_ref, res_ref, rate_ref, out_ref, small_sem, grad_sem, in_sem, out_sem,
    own, pair, joined, incoming, outgoing, decay_pow, decay, tail_high, tail_low, tail, lag_sums,
    partial, from_seq, seq_sum, from_ctx,
    pair_send, pair_recv, chain_send, chain_recv, seq_send, seq_recv, ctx_send, ctx_recv,
):
    rows, width = grad_ref.shape
    modes, groups = res_ref.shape
    per_group = width // groups
    tile_groups = modes if modes * per_group == 256 else 256 // per_group
    tile = tile_groups * per_group
    tiles = width // tile
    chunk_tiles = tiles // chunks
    half = 128
    half_groups = half // per_group
    stacked = tile_groups * modes
    pairs = shards // 2

    span = width // chunks
    rate_copy = pltpu.make_async_copy(rate_hbm, rate_ref, small_sem.at[0])
    res_copy = pltpu.make_async_copy(res_hbm, res_ref, small_sem.at[1])
    in_copy = pltpu.make_async_copy(in_hbm, in_ref, in_sem)
    grad_copies = [
        pltpu.make_async_copy(
            grad_hbm.at[:, q * span : (q + 1) * span],
            grad_ref.at[:, q * span : (q + 1) * span],
            grad_sem.at[q],
        )
        for q in range(chunks)
    ]
    rate_copy.start()
    for copy in grad_copies:
        copy.start()
    in_copy.start()
    res_copy.start()

    me = lax.axis_index("ctx")
    my_seq = lax.axis_index("seq")
    upper = me % 2
    place = me // 2
    partner = me + 1 - 2 * upper
    hops = pairs - 1 - place

    barrier = pltpu.get_barrier_semaphore()
    for offset in range(1, shards):
        pl.semaphore_signal(
            barrier, inc=1, device_id={"ctx": lax.rem(me + offset, shards)}, device_id_type=MESH
        )
    for offset in range(1, seqs):
        pl.semaphore_signal(
            barrier, inc=1, device_id={"seq": lax.rem(my_seq + offset, seqs)}, device_id_type=MESH
        )

    lane_group = lax.broadcasted_iota(jnp.int32, (modes, tile), 1) // per_group
    ahead = lax.broadcasted_iota(jnp.int32, (modes, rows), 1).astype(F32)
    behind = float(rows) - ahead

    def rolled(values, index):
        return pltpu.roll(values, lax.rem(groups - index * tile_groups, groups), 1)

    def compress(wide):
        kept = jnp.zeros((modes, tile), F32)
        for g in range(tile_groups):
            kept = jnp.where(lane_group == g, wide[g * modes : (g + 1) * modes, :], kept)
        return kept

    def lanes(index, size):
        return pl.ds(pl.multiple_of(index * size, size), size)

    def pair_copy(q):
        return pltpu.make_async_remote_copy(
            own.at[q], pair.at[q], pair_send.at[q], pair_recv.at[q],
            device_id={"ctx": partner}, device_id_type=MESH,
        )

    def chain_copy(q):
        return pltpu.make_async_remote_copy(
            outgoing.at[q], incoming.at[q], chain_send.at[q], chain_recv.at[q],
            device_id={"ctx": lax.rem(me + shards - 2, shards)}, device_id_type=MESH,
        )

    rate_copy.wait()
    for q in range(chunks):
        grad_copies[q].wait()

        def summarize(step, carry, q=q):
            index = q * chunk_tiles + step
            rates = rolled(rate_ref[...], index)
            spread = jnp.zeros((modes, tile), F32)
            parts = []
            for g in range(tile_groups):
                rate = rates[:, g : g + 1]
                parts.append(jnp.exp(-rate * ahead))
                spread = jnp.where(lane_group == g, rate, spread)
            decays = jnp.concatenate(parts, axis=0)
            decay[lanes(index, stacked), :] = decays
            high, low = split(decays)
            grads = grad_ref[:, lanes(index, tile)]
            wide = dot(jnp.concatenate([high, low], axis=1), jnp.concatenate([grads, grads], axis=0))
            own[q, :, lanes(step, tile)] = compress(wide)
            decay_pow[q, :, lanes(step, tile)] = jnp.exp(-float(rows) * spread)
            return carry

        lax.fori_loop(0, chunk_tiles, summarize, 0, unroll=True)
        if q == 0:
            pl.semaphore_wait(barrier, shards - 1 + seqs - 1)
        pair_copy(q).start()

    in_copy.wait()
    res_copy.wait()

    def exchange(step):
        @pl.when(step < chunks)
        def _():
            pair_copy(step).wait_recv()
            power = decay_pow[step]
            mine, other = own[step], pair[step]
            near = jnp.where(upper == 0, mine, other)
            far = jnp.where(upper == 0, other, mine)
            joined[step] = near + power * far

            @pl.when(hops == 0)
            def _():
                incoming[step] = jnp.zeros(incoming.shape[1:], F32)
                if pairs > 1:
                    outgoing[step] = joined[step]
                    chain_copy(step).start()

        if pairs > 1:
            q = step - hops

            @pl.when((hops > 0) & (q >= 0) & (q < chunks))
            def _():
                chain_copy(q).wait_recv()

                @pl.when(place > 0)
                def _():
                    power = decay_pow[q]
                    outgoing[q] = joined[q] + power * power * incoming[q]
                    chain_copy(q).start()

    steps = chunks + pairs - 1
    per_step = max(1, tiles // steps)

    sub = min(16, rows)
    subs = rows // sub
    sub_lane_group = lax.broadcasted_iota(jnp.int32, (sub, half), 1) // per_group
    folded_group = lax.rem(
        lax.broadcasted_iota(jnp.int32, (sub, subs * half), 1), half
    ) // per_group
    row_of = lax.broadcasted_iota(jnp.int32, (rows, rows), 0)
    col_of = lax.broadcasted_iota(jnp.int32, (rows, rows), 1)
    sub_row = lax.broadcasted_iota(jnp.int32, (sub, rows), 0)
    sub_col = lax.broadcasted_iota(jnp.int32, (sub, rows), 1)
    causal = sub_col >= sub_row
    inside = sub_col <= rows - sub + sub_row
    mirrored = (row_of // sub == col_of // sub) & (
        lax.rem(row_of, sub) + lax.rem(col_of, sub) == sub - 1
    )
    reverse = jnp.where(mirrored, 1.0, 0.0).astype(BF16)
    group_lane = lax.broadcasted_iota(jnp.int32, (modes, groups), 1)
    amplitude = res_ref[...] * jnp.sqrt(one_minus_exp(2.0 * rate_ref[...]) * (1.0 / modes))
    lag_sums[...] = jnp.zeros_like(lag_sums)

    def convolve(index, carry):
        rates = rolled(rate_ref[...], index)
        amps = rolled(amplitude, index)
        tails = []
        weights = []
        sums = lag_sums[...]
        for part in range(tile // half):
            where_half = lanes(index * (tile // half) + part, half)
            grads = grad_ref[:, where_half]
            ins = dot(reverse, in_ref[:, where_half]).astype(BF16)
            shifted = jnp.concatenate(
                [grads]
                + [
                    jnp.concatenate(
                        [grads[r * sub :], jnp.zeros((r * sub, half), BF16)], axis=0
                    )
                    for r in range(1, subs)
                ],
                axis=1,
            )
            folded = jnp.concatenate([ins[r * sub : (r + 1) * sub] for r in range(subs)], axis=1)
            filters, masked, kept = [], [], []
            for g8 in range(half_groups):
                g = part * half_groups + g8
                rate = rates[:, g : g + 1]
                amp = amps[:, g : g + 1]
                decays = decay[pl.ds(pl.multiple_of(index * stacked + g * modes, modes), modes), :]
                kept.append(decays)
                filt = jnp.sum(amp * decays, axis=0, keepdims=True)
                toeplitz = pltpu.roll(
                    jnp.broadcast_to(filt, (sub, rows)), 0, 1, stride=1, stride_axis=0
                )
                high, low = split(jnp.where(causal, toeplitz, 0.0))
                filters.append(jnp.concatenate([high, low], axis=1))
                masked.append(jnp.where(folded_group == g8, folded, jnp.zeros_like(folded)))
                remaining = jnp.exp(-rate * behind)
                tails.append(remaining)
                weights.append(amp * remaining)
            wide = dot(jnp.concatenate(filters, axis=0), jnp.concatenate([shifted, shifted], axis=0))
            for r in range(subs):
                result = jnp.zeros((sub, half), F32)
                for g8 in range(half_groups):
                    piece = wide[g8 * sub : (g8 + 1) * sub, r * half : (r + 1) * half]
                    result = jnp.where(sub_lane_group == g8, piece, result)
                out_ref[r * sub : (r + 1) * sub, where_half] = result
            products = lax.dot_general(
                jnp.concatenate(masked, axis=0), shifted, (((1,), (1,)), ((), ())),
                preferred_element_type=F32,
            )
            for g8 in range(half_groups):
                g = part * half_groups + g8
                skewed = pltpu.roll(
                    products[g8 * sub : (g8 + 1) * sub], rows + 1 - sub, 1, stride=1, stride_axis=0
                )
                lagged = jnp.sum(jnp.where(inside, skewed, 0.0), axis=0, keepdims=True)
                value = jnp.sum(kept[g8] * lagged, axis=1, keepdims=True)
                sums = jnp.where(group_lane == index * tile_groups + g, value, sums)
        lag_sums[...] = sums
        high, low = split(jnp.concatenate(tails, axis=0))
        ins = in_ref[:, lanes(index, tile)]
        wide = dot(jnp.concatenate([high, low], axis=1), jnp.concatenate([ins, ins], axis=0))
        tail[:, lanes(index, tile)] = compress(wide)
        high, low = split(jnp.concatenate(weights, axis=0).T)
        tail_high[index] = high
        tail_low[index] = low

        return carry

    def advance(step, carry):
        for inner in range(per_step):
            convolve(step * per_step + inner, 0)
        exchange(step)
        return carry

    lax.fori_loop(0, tiles // per_step, advance, 0)
    for index in range(tiles // per_step * per_step, tiles):
        convolve(index, 0)
    for step in range(tiles // per_step, steps):
        exchange(step)

    def enter(index, sums):
        q, inner = index // chunk_tiles, lax.rem(index, chunk_tiles)
        entry = incoming[q, :, lanes(inner, tile)]
        power = decay_pow[q, :, lanes(inner, tile)]
        entry = jnp.where(upper == 0, pair[q, :, lanes(inner, tile)] + power * entry, entry)
        incoming[q, :, lanes(inner, tile)] = entry
        value = tail[:, lanes(index, tile)] * entry
        high = value.astype(BF16)
        rest = value - high.astype(F32)
        middle, low = split(rest)
        chan_group = lax.broadcasted_iota(jnp.int32, (tile, groups), 0) // per_group
        member = lax.broadcasted_iota(jnp.int32, (tile, groups), 1) == chan_group + index * tile_groups
        member = jnp.where(member, 1.0, 0.0).astype(BF16)
        found = dot(jnp.concatenate([high, middle, low], axis=0), member)
        return sums + found[:modes] + found[modes : 2 * modes] + found[2 * modes :]

    partial[...] = lax.fori_loop(0, tiles, enter, lag_sums[...], unroll=4)

    def seq_copy(offset):
        return pltpu.make_async_remote_copy(
            partial, from_seq.at[offset - 1], seq_send.at[offset - 1], seq_recv.at[offset - 1],
            device_id={"seq": lax.rem(my_seq + offset, seqs)}, device_id_type=MESH,
        )

    def ctx_copy(offset):
        return pltpu.make_async_remote_copy(
            seq_sum, from_ctx.at[offset - 1], ctx_send.at[offset - 1], ctx_recv.at[offset - 1],
            device_id={"ctx": lax.rem(me + offset, shards)}, device_id_type=MESH,
        )

    for offset in range(1, seqs):
        seq_copy(offset).start()

    def carry_in(index, carry):
        q, inner = index // chunk_tiles, lax.rem(index, chunk_tiles)
        entry = incoming[q, :, lanes(inner, tile)]
        high, low = split(entry)

        def blocks(value):
            return jnp.concatenate(
                [jnp.where(lane_group == g, value, jnp.zeros_like(value)) for g in range(tile_groups)],
                axis=0,
            )

        left = tail_high[index]
        both = dot(jnp.concatenate([left, tail_low[index]], axis=0), blocks(high))
        rest = dot(left, blocks(low))
        out_ref[:, lanes(index, tile)] += both[:rows] + both[rows:] + rest
        return carry

    def out_copy(q):
        return pltpu.make_async_copy(
            out_ref.at[:, q * span : (q + 1) * span],
            out_hbm.at[:, q * span : (q + 1) * span],
            out_sem.at[q],
        )

    def finish(q):
        lax.fori_loop(q * chunk_tiles, (q + 1) * chunk_tiles, carry_in, 0, unroll=True)
        out_copy(q).start()

    for q in range(chunks // 2):
        finish(q)
    for offset in range(1, seqs):
        seq_copy(offset).wait_recv()

    def ordered(mine, received, place_here, count):
        added = jnp.zeros((modes, groups), F32)
        for source in range(count):
            value = jnp.where(place_here == source, mine, 0.0)
            for offset in range(1, count):
                value = jnp.where(
                    lax.rem(source + offset, count) == place_here, received[offset - 1], value
                )
            added = added + value
        return added

    seq_sum[...] = ordered(partial[...], from_seq, my_seq, seqs)
    for offset in range(1, shards):
        ctx_copy(offset).start()
    for q in range(chunks // 2, chunks):
        finish(q)
    for offset in range(1, shards):
        ctx_copy(offset).wait_recv()

    def gather_sum(source, added):
        offset = lax.rem(me - source + shards, shards)
        slot = jnp.maximum(offset - 1, 0)
        return added + jnp.where(offset == 0, seq_sum[...], from_ctx[slot])

    total = lax.fori_loop(0, shards, gather_sum, jnp.zeros((modes, groups), F32))
    scale = 1.0 / float(seqs * shards * rows * per_group)
    total_ref[...] = total * jnp.sqrt(one_minus_exp(2.0 * rate_ref[...]) * scale)

    for q in range(chunks):
        out_copy(q).wait()
        pair_copy(q).wait_send()
        if pairs > 1:
            @pl.when(place > 0)
            def _(q=q):
                chain_copy(q).wait_send()
    for offset in range(1, seqs):
        seq_copy(offset).wait_send()
    for offset in range(1, shards):
        ctx_copy(offset).wait_send()


def local(shards, seqs, grad_out, inputs, residues, rates):
    rows, width = grad_out.shape[1:]
    modes, groups = residues.shape
    chunks = 4
    tile = 256
    chunk_shape = (chunks, modes, width // chunks)
    small = (modes, groups)
    states = pltpu.VMEM(chunk_shape, F32)
    dma = pltpu.SemaphoreType.DMA
    vmem = pl.BlockSpec(memory_space=pltpu.VMEM)
    grad_in, total = pl.pallas_call(
        functools.partial(body, shards, seqs, chunks),
        out_shape=(
            jax.ShapeDtypeStruct((rows, width), F32),
            jax.ShapeDtypeStruct(small, F32),
        ),
        in_specs=[pl.BlockSpec(memory_space=pltpu.HBM)] * 4,
        out_specs=(pl.BlockSpec(memory_space=pltpu.HBM), vmem),
        scratch_shapes=[
            pltpu.VMEM((rows, width), BF16), pltpu.VMEM((rows, width), BF16),
            pltpu.VMEM(small, F32), pltpu.VMEM(small, F32), pltpu.VMEM((rows, width), F32),
            dma((2,)), dma((chunks,)), dma, dma((chunks,)),
            states, states, states, states, states, states,
            pltpu.VMEM((groups * modes, rows), F32),
            pltpu.VMEM((width // tile, rows, tile // (width // groups) * modes), BF16),
            pltpu.VMEM((width // tile, rows, tile // (width // groups) * modes), BF16),
            pltpu.VMEM((modes, width), F32),
            pltpu.VMEM(small, F32),
            pltpu.VMEM(small, F32),
            pltpu.VMEM((seqs - 1,) + small, F32),
            pltpu.VMEM(small, F32),
            pltpu.VMEM((shards - 1,) + small, F32),
            dma((chunks,)), dma((chunks,)), dma((chunks,)), dma((chunks,)),
            dma((seqs - 1,)), dma((seqs - 1,)), dma((shards - 1,)), dma((shards - 1,)),
        ],
        compiler_params=pltpu.CompilerParams(
            collective_id=0, has_side_effects=True, vmem_limit_bytes=63 * 1024 * 1024
        ),
    )(grad_out[0], inputs[0], residues, rates)
    return grad_in[None], total


def solution(mesh):
    placed = (P("seq", "ctx", None), P("seq", "ctx", None), P(), P())
    return jax.shard_map(
        functools.partial(local, mesh.shape["ctx"], mesh.shape["seq"]),
        mesh=mesh, in_specs=placed, out_specs=(P("seq", "ctx", None), P()), check_vma=False,
    )
```
